128 devices in a mesh: lat: 8 (over x, core), lon: 16 (over y, z).
Axes of the slice: x: 4, y: 4, z: 4, core: 2. Of those that a mesh axis runs over, the one named last changes fastest.
Arguments:
- species: float32 [4096, 48, 128], P(('lat', 'lon')), may hold values from -6 to 6
- reaction_rates: float32 [48, 48], replicated, may hold values from -0.875 to 0.875
- mix_rate: float32 [48], replicated, may hold values from 0.05 to 0.9
- shift_list: int32 [2, 8, 32], P(None, 'lat'), may hold values from -2 to 2, as said below
- arrival: int32 [2, 4096], P(None, ('lat', 'lon')), may hold values from 0 to 31, as said below
- cell_index: int32 [2, 4096, 128], P(None, ('lat', 'lon')), may hold values from 0 to 131071, as said below
Outputs:
- final_species: float32 [4096, 48, 128], P(('lat', 'lon'))
The draws below stay inside these ranges and needn't reach their ends.
Inputs may be any that keep to these rules, and one draw needn't show every extreme that they name: `shift_list`: in every step the first and last band move exactly 8 slots by +1 and by -1 sector and 4 slots by +2 and by -2; the other bands half of each; all other slots stay. Which slots is random. `arrival`: each device's 32 entries of a step are a permutation of its slots. `cell_index`: A parcel's cell is owned (cell // 1024 in band-major order) by its own device or one of the eight beside it; bands do not wrap, sectors wrap.
All inputs are finite; a program needn't handle non-finite values.
Results may differ from the reference program's by a relative error of at most 0.0001.
Values sent between devices are 32-bit elements; how exact they have to be, the bound alone decides.
A program may use at most 64 MiB of HBM per device.

```python
import math
import jax
import jax.numpy as jnp
from jax import lax

S = 48
P_SIZE = 128
BLK_DEV = 32
CELL_DEV = 1024
STEPS = 2
SUB = 32
BANDS = 8
SECTORS = 16
BLOCKS = 4096
CELLS = 131072
MOST = 8


def draw_shift_list(key, part):
    key = jax.random.fold_in(key, 11)
    total_rows = STEPS * BANDS
    row_keys = jax.random.split(key, total_rows)
    positions = jax.vmap(lambda subkey: jax.random.permutation(subkey, BLK_DEV))(row_keys)
    band_ids = jnp.arange(total_rows, dtype=jnp.int32) % BANDS
    polar = (band_ids == 0) | (band_ids == BANDS - 1)
    near_count = jnp.where(polar, MOST, MOST // 2)[:, None]
    far_count = jnp.where(polar, MOST // 2, MOST // 4)[:, None]
    values = jnp.where(positions < near_count, 1, jnp.where(positions < 2 * near_count, -1, jnp.where(positions < 2 * near_count + far_count, 2, jnp.where(positions < 2 * near_count + 2 * far_count, -2, 0))))
    return values.reshape(STEPS, BANDS, BLK_DEV).astype(jnp.int32)


def draw_arrival(key, part):
    key = jax.random.fold_in(key, 12)
    device_count = BLOCKS // BLK_DEV
    row_keys = jax.random.split(key, STEPS * device_count)
    perms = jax.vmap(lambda subkey: jax.random.permutation(subkey, BLK_DEV))(row_keys)
    return perms.reshape(STEPS, BLOCKS).astype(jnp.int32)


def draw_cell_index(key, part):
    key = jax.random.fold_in(key, 13)
    first_key, second_key, third_key = jax.random.split(key, 3)
    shape = (STEPS, BLOCKS, P_SIZE)
    block_ids = jax.lax.broadcasted_iota(jnp.int32, shape, 1)
    device_ids = block_ids // BLK_DEV
    band_ids = device_ids // SECTORS
    sector_ids = device_ids % SECTORS
    band_step = jax.random.randint(first_key, shape, -1, 2)
    sector_step = jax.random.randint(second_key, shape, -1, 2)
    new_band = jnp.clip(band_ids + band_step, 0, BANDS - 1)
    new_sector = (sector_ids + sector_step) % SECTORS
    local_cell = jax.random.randint(third_key, shape, 0, CELL_DEV)
    return ((new_band * SECTORS + new_sector) * CELL_DEV + local_cell).astype(jnp.int32)


def shard_levels(key, extent, pieces, least, top_value):
    def one(position, parts):
        heights = jax.random.uniform(jax.random.fold_in(jax.random.fold_in(key, 6), position), (parts,), jnp.float32, least / len(pieces), top_value / len(pieces))
        return jnp.repeat(jnp.exp(heights), extent[position] // parts).reshape((-1,) + (1,) * (len(extent) - position - 1))

    factor_of = one(*pieces[0])
    for cut in pieces[1:]:
        factor_of = factor_of * one(*cut)
    return factor_of


def bell_draw(key, shape, deviation, bound, pieces=(), kind=jnp.bfloat16):
    result = jax.random.normal(key, shape, jnp.float32) * deviation
    if len(pieces) > 0:
        result = shard_levels(key, shape, pieces, -0.22, 0.18) * result
    return jnp.clip(result, min=-bound, max=bound).astype(kind)


def setup_inputs(seed: int = 0) -> dict:
    arg_keys = jax.random.split(jax.random.key(seed), 7)
    species = bell_draw(arg_keys[0], (BLOCKS, S, P_SIZE), 1.0, 6.0, ((0, 128),), jnp.float32)
    reaction_rates = bell_draw(arg_keys[1], (S, S), S ** -0.5, 0.875, (), jnp.float32)
    mix_rate = jnp.clip(jnp.exp(jax.random.uniform(arg_keys[2], (S,), jnp.float32, math.log(0.05), math.log(0.9))), 0.05, 0.9)
    shift_list = draw_shift_list(jax.random.fold_in(arg_keys[6], 71), 0)
    arrival = draw_arrival(jax.random.fold_in(arg_keys[6], 71), 0)
    cell_index = draw_cell_index(jax.random.fold_in(arg_keys[6], 71), 0)
    return dict(species=species, reaction_rates=reaction_rates, mix_rate=mix_rate, shift_list=shift_list, arrival=arrival, cell_index=cell_index)


def chemistry(state, reaction_rates):
    substep = 2.0 / SUB

    def advance(counter, current):
        pushed = jnp.einsum("st,btp->bsp", reaction_rates, current, precision=lax.Precision.HIGHEST)
        return current + substep * jnp.tanh(pushed)

    return lax.fori_loop(0, SUB, advance, state)


def reference(species, reaction_rates, mix_rate, shift_list, arrival, cell_index):
    state = species
    slot_ids = jnp.arange(BLOCKS, dtype=jnp.int32)
    owner_dev = slot_ids // BLK_DEV
    own_band = owner_dev // SECTORS
    own_sector = owner_dev % SECTORS
    for section in range(STEPS):
        old_slot = arrival[section].astype(jnp.int32)
        moved_by = shift_list[section][own_band, old_slot]
        source = (own_band * SECTORS + (own_sector - moved_by) % SECTORS) * BLK_DEV + old_slot
        moved = state[source.astype(jnp.int32)]
        chem = chemistry(moved, reaction_rates)
        cell_ids = cell_index[section].reshape(-1)
        flat_state = moved.transpose(1, 0, 2).reshape(S, BLOCKS * P_SIZE)
        cell_sums = jnp.zeros((S, CELLS), jnp.float32).at[:, cell_ids].add(flat_state)
        cell_counts = jnp.zeros((CELLS,), jnp.float32).at[cell_ids].add(1.0)
        cell_means = cell_sums / jnp.maximum(cell_counts, 1.0)
        picked = cell_means[:, cell_ids].reshape(S, BLOCKS, P_SIZE).transpose(1, 0, 2)
        state = chem + mix_rate[None, :, None] * (picked - moved)
    return state
```

```python
import functools

import jax
import jax.numpy as jnp
from jax import lax
from jax.experimental import pallas as pl
from jax.experimental.pallas import tpu as pltpu
from jax.sharding import PartitionSpec as P

S = 48
LANES = 128
BLK = 32
CELL_DEV = 1024
ROWS = CELL_DEV // 2
STEPS = 2
SUB = 32
MOST = 8
BASES = (0, 8, 16, 20)
SIZES = (8, 8, 4, 4)
OFFSETS = (1, -1, 2, -2)
OUTGOING = 24
ACCS = 4
CHUNKS = 2
CHUNK = ROWS // CHUNKS
F32 = jnp.float32
BF16 = jnp.bfloat16
MESH = pl.DeviceIdType.MESH
VMEM = pl.BlockSpec(memory_space=pltpu.VMEM)
SMEM = pl.BlockSpec(memory_space=pltpu.SMEM)
LIMIT = 48 * 2**20


def around(axis, step):
    count = lax.axis_size(axis)
    return lax.rem(lax.axis_index(axis) + step + count, count)


def prepare_kernel(shift_ref, arrival_ref, place_ref, cell_ref, send_ref, source_ref, row_ref, half_ref, pool_ref):
    band = place_ref[0]
    sector = place_ref[1]
    cell = cell_ref[...]
    owner = cell // CELL_DEV
    rel_band = owner // 16 - band + 1
    rel_sector = (owner % 16 - sector + 17) % 16
    row_ref[...] = jnp.clip((rel_band * 3 + rel_sector) * ROWS + cell % ROWS, 0, 9 * ROWS - 1)
    half_ref[...] = (cell // ROWS) % 2
    for step in range(STEPS):
        for k in range(OUTGOING):
            send_ref[step, k] = 0

        def place(slot, counts):
            moved_by = shift_ref[step, 0, slot]
            pool = slot
            later = []
            for offset, base, size, count in zip(OFFSETS, BASES, SIZES, counts):
                hit = moved_by == offset
                where = base + jnp.minimum(count, size - 1)

                @pl.when(hit)
                def _():
                    send_ref[step, where] = slot

                pool = jnp.where(hit, BLK + where, pool)
                later.append(count + hit.astype(jnp.int32))
            pool_ref[slot] = pool
            return tuple(later)

        lax.fori_loop(0, BLK, place, (jnp.int32(0),) * 4)

        @pl.loop(0, BLK)
        def _(slot):
            source_ref[step, slot] = pool_ref[arrival_ref[step, slot]]


def prepare(shift_list, arrival, cell_index):
    place = jnp.stack([lax.axis_index("lat"), lax.axis_index("lon")]).astype(jnp.int32)
    return pl.pallas_call(
        prepare_kernel,
        out_shape=(
            jax.ShapeDtypeStruct((STEPS, OUTGOING), jnp.int32),
            jax.ShapeDtypeStruct((STEPS, BLK), jnp.int32),
            jax.ShapeDtypeStruct((STEPS, BLK, LANES), jnp.int32),
            jax.ShapeDtypeStruct((STEPS, BLK, LANES), jnp.int32),
        ),
        in_specs=[SMEM, SMEM, SMEM, VMEM],
        out_specs=(SMEM, SMEM, VMEM, VMEM),
        scratch_shapes=[pltpu.SMEM((BLK,), jnp.int32)],
        name="prepare",
    )(shift_list, arrival, place, cell_index)


def migrate_kernel(send_ref, source_ref, state_ref, moved_ref, outgoing, pool, send_sem, recv_sem):
    band = lax.axis_index("lat")
    polar = (band == 0) | (band == lax.axis_size("lat") - 1)
    barrier = pltpu.get_barrier_semaphore()
    for offset in OFFSETS:
        pl.semaphore_signal(barrier, inc=1, device_id={"lon": around("lon", offset)}, device_id_type=MESH)

    for k in range(OUTGOING):
        outgoing[k] = state_ref[send_ref[k]]
    pl.semaphore_wait(barrier, len(OFFSETS))

    def copies(share):
        return [
            pltpu.make_async_remote_copy(
                src_ref=outgoing.at[pl.ds(base, size // share)],
                dst_ref=pool.at[pl.ds(BLK + base, size // share)],
                send_sem=send_sem.at[d],
                recv_sem=recv_sem.at[d],
                device_id={"lon": around("lon", offset)},
                device_id_type=MESH,
            )
            for d, (offset, base, size) in enumerate(zip(OFFSETS, BASES, SIZES))
        ]

    def exchange(share):
        moving = copies(share)
        for copy in moving:
            copy.start()
        pool[0:BLK] = state_ref[...]
        for copy in moving:
            copy.wait()

    @pl.when(polar)
    def _():
        exchange(1)

    @pl.when(jnp.logical_not(polar))
    def _():
        exchange(2)

    @pl.loop(0, BLK, unroll=4)
    def _(slot):
        moved_ref[slot] = pool[source_ref[slot]]


def migrate(send, source, state):
    return pl.pallas_call(
        migrate_kernel,
        out_shape=jax.ShapeDtypeStruct((BLK, S, LANES), F32),
        in_specs=[SMEM, SMEM, VMEM],
        out_specs=VMEM,
        scratch_shapes=[
            pltpu.VMEM((OUTGOING, S, LANES), F32),
            pltpu.VMEM((BLK + OUTGOING, S, LANES), F32),
            pltpu.SemaphoreType.DMA((4,)),
            pltpu.SemaphoreType.DMA((4,)),
        ],
        compiler_params=pltpu.CompilerParams(collective_id=1, has_side_effects=True, vmem_limit_bytes=LIMIT),
        name="migrate",
    )(send, source, state)


def deposit_kernel(moved_ref, half_ref, row_ref, sums_ref, rows, *accs):
    blank = jnp.zeros((8, LANES), F32)
    tail = jnp.where(lax.broadcasted_iota(jnp.int32, (16, LANES), 0) == 0, 1.0, 0.0)

    @pl.loop(0, 9 * ROWS // 8, unroll=8)
    def _(i):
        part = pl.ds(pl.multiple_of(i * 8, 8), 8)
        for acc in accs:
            acc[part, :] = blank

    @pl.loop(0, BLK, unroll=2)
    def _(b):
        block = jnp.concatenate([moved_ref[b], tail], 0)
        half = half_ref[pl.ds(b, 1), :]
        both = jnp.concatenate([jnp.where(half == 0, block, 0.0), jnp.where(half == 0, 0.0, block)], 0)
        rows[pl.ds(pl.multiple_of(b * LANES, LANES), LANES), :] = both.T

    @pl.loop(0, BLK)
    def _(b):
        @pl.loop(0, LANES // 32)
        def _(g):
            first = g * 32
            start = pl.multiple_of(b * LANES + first, 32)
            for k in range(32):
                acc = accs[k % ACCS]
                at = pl.ds(row_ref[b, first + k], 1)
                acc[at, :] = acc[at, :] + rows[pl.ds(start + k, 1), :]

    @pl.loop(0, 9 * ROWS // 8, unroll=4)
    def _(i):
        part = pl.ds(pl.multiple_of(i * 8, 8), 8)
        total = accs[0][part, :]
        for acc in accs[1:]:
            total = total + acc[part, :]
        sums_ref[part, :] = total


def deposit(moved, half, row):
    sums = pl.pallas_call(
        deposit_kernel,
        out_shape=jax.ShapeDtypeStruct((9 * ROWS, LANES), F32),
        in_specs=[VMEM, VMEM, SMEM],
        out_specs=VMEM,
        scratch_shapes=[pltpu.VMEM((BLK * LANES, LANES), F32)] + [pltpu.VMEM((9 * ROWS, LANES), F32)] * ACCS,
        compiler_params=pltpu.CompilerParams(vmem_limit_bytes=LIMIT),
        name="deposit",
    )(moved, half, row)
    return sums.reshape(3, 3, ROWS, LANES)


def split(x):
    high = x.astype(BF16)
    return high, (x - high.astype(F32)).astype(BF16)


def pairs_of(rates):
    zero = jnp.zeros((S, S), F32)
    high, low = split(jnp.concatenate([jnp.concatenate([rates, zero], 1), jnp.concatenate([zero, rates], 1)], 0))
    return jnp.concatenate([high, high], 1), low


def exchange_kernel(
    sums_ref, moved_ref, rates_ref, mix_ref, half_ref, row_ref, out_ref,
    below, above, middle, left, right, table, chem, high2, low1, rows,
    up_sem, down_sem, west_sem, east_sem, mwest_sem, meast_sem, mup_sem, mdown_sem,
):
    band = lax.axis_index("lat")
    bands = lax.axis_size("lat")
    has_up = band < bands - 1
    has_down = band > 0
    up = jnp.minimum(band + 1, bands - 1)
    down = jnp.maximum(band - 1, 0)
    east = around("lon", 1)
    west = around("lon", -1)
    barrier = pltpu.get_barrier_semaphore()
    for sector in (east, west):
        pl.semaphore_signal(barrier, inc=1, device_id={"lon": sector}, device_id_type=MESH)

    @pl.when(has_up)
    def _():
        pl.semaphore_signal(barrier, inc=1, device_id={"lat": up}, device_id_type=MESH)

    @pl.when(has_down)
    def _():
        pl.semaphore_signal(barrier, inc=1, device_id={"lat": down}, device_id_type=MESH)

    pl.semaphore_wait(barrier, 2 + has_up.astype(jnp.int32) + has_down.astype(jnp.int32))

    def remote(src, dst, sem, index, device):
        return pltpu.make_async_remote_copy(
            src_ref=src, dst_ref=dst, send_sem=sem.at[(0,) + index], recv_sem=sem.at[(1,) + index],
            device_id=device, device_id_type=MESH,
        )

    def chunk(c):
        return pl.ds(c * CHUNK, CHUNK)

    def sums_up(s, c):
        return remote(sums_ref.at[2, s, chunk(c)], below.at[s, chunk(c)], up_sem, (s, c), {"lat": up})

    def sums_down(s, c):
        return remote(sums_ref.at[0, s, chunk(c)], above.at[s, chunk(c)], down_sem, (s, c), {"lat": down})

    def sums_west(c):
        return remote(middle.at[0, chunk(c)], right.at[chunk(c)], west_sem, (c,), {"lon": west})

    def sums_east(c):
        return remote(middle.at[2, chunk(c)], left.at[chunk(c)], east_sem, (c,), {"lon": east})

    def means_west(c):
        return remote(table.at[1, 1, chunk(c)], table.at[1, 2, chunk(c)], mwest_sem, (c,), {"lon": west})

    def means_east(c):
        return remote(table.at[1, 1, chunk(c)], table.at[1, 0, chunk(c)], meast_sem, (c,), {"lon": east})

    def means_up(s, c):
        return remote(table.at[1, s, chunk(c)], table.at[0, s, chunk(c)], mup_sem, (s, c), {"lat": up})

    def means_down(s, c):
        return remote(table.at[1, s, chunk(c)], table.at[2, s, chunk(c)], mdown_sem, (s, c), {"lat": down})

    order = [(s, c) for c in range(CHUNKS) for s in (0, 2, 1)]

    @pl.when(has_up)
    def _():
        for s, c in order:
            sums_up(s, c).start()

    @pl.when(has_down)
    def _():
        for s, c in order:
            sums_down(s, c).start()

    @pl.when(jnp.logical_not(has_down))
    def _():
        below[...] = jnp.zeros_like(below)
        table[0] = jnp.zeros_like(table[0])

    @pl.when(jnp.logical_not(has_up))
    def _():
        above[...] = jnp.zeros_like(above)
        table[2] = jnp.zeros_like(table[2])

    high, low = pairs_of(rates_ref[...])
    high2[...] = high
    low1[...] = low
    for b in range(BLK):
        chem[(b % 2) * S:(b % 2) * S + S, (b // 2) * LANES:(b // 2 + 1) * LANES] = moved_ref[b]

    def chemistry(substeps):
        def advance(_, current):
            state = chem[...]
            high, low = split(state)
            pushed = jnp.dot(high2[...], jnp.concatenate([high, low], 0), preferred_element_type=F32)
            pushed = pushed + jnp.dot(low1[...], high, preferred_element_type=F32)
            chem[...] = state + (2.0 / SUB) * jnp.tanh(pushed)
            return current

        lax.fori_loop(0, substeps, advance, 0)

    def strips(body):
        @pl.loop(0, CHUNK // 8, unroll=4)
        def _(i):
            body(pl.multiple_of(i * 8, 8))

    chemistry(12)
    for c in range(CHUNKS):
        for s in (0, 2, 1):
            @pl.when(has_down)
            def _():
                sums_up(s, c).wait_recv()

            @pl.when(has_up)
            def _():
                sums_down(s, c).wait_recv()

            def add_bands(i):
                part = pl.ds(c * CHUNK + i, 8)
                middle[s, part, :] = sums_ref[1, s, part, :] + below[s, part, :] + above[s, part, :]

            strips(add_bands)
            if s == 0:
                sums_west(c).start()
            if s == 2:
                sums_east(c).start()

    chemistry(10)
    lane = lax.broadcasted_iota(jnp.int32, (8, LANES), 1)
    for c in range(CHUNKS):
        sums_west(c).wait_recv()
        sums_east(c).wait_recv()

        def mean(i):
            part = pl.ds(c * CHUNK + i, 8)
            total = middle[1, part, :] + left[part, :] + right[part, :]
            count = jnp.where(lane < 64, total[:, S:S + 1], total[:, 64 + S:64 + S + 1])
            table[1, 1, part, :] = total / jnp.maximum(count, 1.0)

        strips(mean)
        means_west(c).start()
        means_east(c).start()

        @pl.when(has_up)
        def _():
            means_up(1, c).start()

        @pl.when(has_down)
        def _():
            means_down(1, c).start()

    chemistry(5)
    for c in range(CHUNKS):
        means_west(c).wait_recv()
        means_east(c).wait_recv()

        @pl.when(has_up)
        def _():
            means_up(0, c).start()
            means_up(2, c).start()

        @pl.when(has_down)
        def _():
            means_down(0, c).start()
            means_down(2, c).start()

    chemistry(5)
    for s, c in order:
        @pl.when(has_up)
        def _():
            means_down(s, c).wait_recv()
            sums_up(s, c).wait_send()
            means_up(s, c).wait_send()

        @pl.when(has_down)
        def _():
            means_up(s, c).wait_recv()
            sums_down(s, c).wait_send()
            means_down(s, c).wait_send()
    for c in range(CHUNKS):
        for copy in (sums_west(c), sums_east(c), means_west(c), means_east(c)):
            copy.wait_send()

    @pl.loop(0, BLK)
    def _(b):
        @pl.loop(0, LANES // 32)
        def _(g):
            first = g * 32
            start = pl.multiple_of(b * LANES + first, 32)
            for k in range(32):
                rows[pl.ds(start + k, 1), :] = table_rows(table, row_ref[b, first + k])

    mix = mix_ref[...]

    @pl.loop(0, BLK // 2)
    def _(pair):
        for side in range(2):
            b = pair * 2 + side
            means = rows[pl.ds(pl.multiple_of(b * LANES, LANES), LANES), :].T
            picked = jnp.where(half_ref[pl.ds(b, 1), :] == 0, means[0:S], means[64:64 + S])
            reacted = chem[side * S:side * S + S, pl.ds(pl.multiple_of(pair * LANES, LANES), LANES)]
            out_ref[b] = reacted + mix * (picked - moved_ref[b])


def table_rows(table, at):
    return table.reshape(9 * ROWS, LANES)[pl.ds(at, 1), :]


def exchange(sums, moved, rates, mix, half, row):
    region = (3, ROWS, LANES)
    pair = pltpu.SemaphoreType.DMA((2, 3, CHUNKS))
    single = pltpu.SemaphoreType.DMA((2, CHUNKS))
    return pl.pallas_call(
        exchange_kernel,
        out_shape=jax.ShapeDtypeStruct((BLK, S, LANES), F32),
        in_specs=[VMEM, VMEM, VMEM, VMEM, VMEM, SMEM],
        out_specs=VMEM,
        scratch_shapes=[
            pltpu.VMEM(region, F32),
            pltpu.VMEM(region, F32),
            pltpu.VMEM(region, F32),
            pltpu.VMEM((ROWS, LANES), F32),
            pltpu.VMEM((ROWS, LANES), F32),
            pltpu.VMEM((3, 3, ROWS, LANES), F32),
            pltpu.VMEM((2 * S, BLK // 2 * LANES), F32),
            pltpu.VMEM((2 * S, 4 * S), BF16),
            pltpu.VMEM((2 * S, 2 * S), BF16),
            pltpu.VMEM((BLK * LANES, LANES), F32),
            pair, pair, single, single, single, single, pair, pair,
        ],
        compiler_params=pltpu.CompilerParams(collective_id=2, has_side_effects=True, vmem_limit_bytes=LIMIT),
        name="exchange",
    )(sums, moved, rates, mix, half, row)


def shards(species, reaction_rates, mix_rate, shift_list, arrival, cell_index):
    send, source, row, half = prepare(shift_list, arrival, cell_index)
    mix = jnp.broadcast_to(mix_rate[:, None], (S, LANES))
    state = species
    for step in range(STEPS):
        moved = migrate(send[step], source[step], state)
        sums = deposit(moved, half[step], row[step])
        state = exchange(sums, moved, reaction_rates, mix, half[step], row[step])
    return state


def solution(mesh):
    placed = (
        P(("lat", "lon"), None, None),
        P(),
        P(),
        P(None, "lat", None),
        P(None, ("lat", "lon")),
        P(None, ("lat", "lon"), None),
    )
    return jax.shard_map(
        shards, mesh=mesh, in_specs=placed, out_specs=P(("lat", "lon"), None, None), check_vma=False
    )
```

```python
import functools

import jax
import jax.numpy as jnp
from jax import lax
from jax.experimental import pallas as pl
from jax.experimental.pallas import tpu as pltpu
from jax.sharding import PartitionSpec as P

S = 48
LANES = 128
BLK = 32
CELL_DEV = 1024
ROWS = CELL_DEV // 2
STEPS = 2
SUB = 32
ACCS = 4
CHUNKS = 4
CHUNK = ROWS // CHUNKS
F32 = jnp.float32
BF16 = jnp.bfloat16
MESH = pl.DeviceIdType.MESH
VMEM = pl.BlockSpec(memory_space=pltpu.VMEM)
SMEM = pl.BlockSpec(memory_space=pltpu.SMEM)
LIMIT = 48 * 2**20
BATCHES = (2, -2, 1, 1, -1, -1)
FIRST = {2: 0, -2: 1, 1: 2, -1: 4}
LAST_FIRST = (3, 0, 1, 2)
PLAN = (6, ("a", 3), 2, ("a", 0), 2, ("a", 1), 2, ("b", 3), ("a", 2), 3, ("b", 0), 2, ("b", 1), 2, ("b", 2), 3, ("c", 0), 3, ("c", 1), 3, ("c", 2), 4)


def around(axis, step):
    count = lax.axis_size(axis)
    return lax.rem(lax.axis_index(axis) + step + count, count)


def is_polar():
    band = lax.axis_index("lat")
    return (band == 0) | (band == lax.axis_size("lat") - 1)


def place_slots(shift_ref, step, unit, visit):
    def place(slot, counts):
        moved_by = shift_ref[step, 0, slot]
        where = 6 * unit + counts[4]
        later = []
        for offset, count in zip((2, -2, 1, -1), counts):
            hit = moved_by == offset
            where = jnp.where(hit, FIRST[offset] * unit + count, where)
            later.append(count + hit.astype(jnp.int32))
        later.append(counts[4] + (moved_by == 0).astype(jnp.int32))
        visit(slot, moved_by, jnp.minimum(where, BLK - 1))
        return tuple(later)

    lax.fori_loop(0, BLK, place, (jnp.int32(0),) * 5)


def batch_copy(pool, send_sem, recv_sem, k, unit):
    return pltpu.make_async_remote_copy(
        src_ref=pool.at[pl.ds(k * unit, unit)],
        dst_ref=pool.at[pl.ds(BLK + k * unit, unit)],
        send_sem=send_sem.at[k],
        recv_sem=recv_sem.at[k],
        device_id={"lon": around("lon", BATCHES[k])},
        device_id_type=MESH,
    )


def each_unit(polar, body):
    @pl.when(polar)
    def _():
        body(4)

    @pl.when(jnp.logical_not(polar))
    def _():
        body(2)


def migrate_kernel(shift_ref, arrival_ref, state_ref, cell_ref, moved_ref, row_ref, pool, pool_at, send_sem, recv_sem):
    polar = is_polar()
    unit = jnp.where(polar, 4, 2)
    barrier = pltpu.get_barrier_semaphore()
    for offset in (1, -1, 2, -2):
        pl.semaphore_signal(barrier, inc=1, device_id={"lon": around("lon", offset)}, device_id_type=MESH)

    def note(slot, moved_by, where):
        pool_at[slot] = where + jnp.where(moved_by == 0, 0, BLK)

    place_slots(shift_ref, 0, unit, note)

    @pl.loop(0, 6 * unit)
    def _(where):
        def seek(slot, found):
            return jnp.where(pool_at[slot] == where + BLK, slot, found)

        pool[where] = state_ref[lax.fori_loop(0, BLK, seek, jnp.int32(0), unroll=True)]

    pl.semaphore_wait(barrier, 4)

    def start(unit):
        for k in range(6):
            batch_copy(pool, send_sem, recv_sem, k, unit).start()

    each_unit(polar, start)
    sectors = lax.axis_size("lon")
    cell = cell_ref[...]
    owner = cell // CELL_DEV
    rel_band = owner // sectors - lax.axis_index("lat") + 1
    rel_sector = (owner % sectors - lax.axis_index("lon") + 1 + sectors) % sectors
    row_ref[...] = jnp.clip((rel_band * 3 + rel_sector) * ROWS + cell % ROWS, 0, 9 * ROWS - 1)

    def wait(unit):
        for k in range(6):
            batch_copy(pool, send_sem, recv_sem, k, unit).wait()

    each_unit(polar, wait)

    @pl.loop(0, BLK, unroll=4)
    def _(slot):
        old = arrival_ref[0, slot]
        at = pool_at[old]
        moved_ref[slot] = jnp.where(at < BLK, state_ref[old], pool[at])


def migrate(shift_list, arrival, state, cell_index):
    return pl.pallas_call(
        migrate_kernel,
        out_shape=(jax.ShapeDtypeStruct((BLK, S, LANES), F32), jax.ShapeDtypeStruct((STEPS, BLK, LANES), jnp.int32)),
        in_specs=[SMEM, SMEM, VMEM, VMEM],
        out_specs=(VMEM, VMEM),
        scratch_shapes=[
            pltpu.VMEM((2 * BLK, S, LANES), F32),
            pltpu.SMEM((BLK,), jnp.int32),
            pltpu.SemaphoreType.DMA((6,)),
            pltpu.SemaphoreType.DMA((6,)),
        ],
        compiler_params=pltpu.CompilerParams(collective_id=1, has_side_effects=True, vmem_limit_bytes=LIMIT),
        name="migrate",
    )(shift_list, arrival, state, cell_index)


def deposit_kernel(step, moved_ref, cell_ref, row_ref, shift_ref, arrival_ref, sums_ref, order_ref, source_ref, even, odd, pool_at, *accs):
    blank = jnp.zeros((8, LANES), F32)
    tail = jnp.where(lax.broadcasted_iota(jnp.int32, (16, LANES), 0) == 0, 1.0, 0.0)

    @pl.loop(0, 9 * ROWS // 8, unroll=8)
    def _(i):
        part = pl.ds(pl.multiple_of(i * 8, 8), 8)
        for acc in accs:
            acc[part, :] = blank

    def turn(b, rows):
        block = jnp.concatenate([moved_ref[b], tail], 0)
        low = (cell_ref[step, pl.ds(b, 1), :] & ROWS) == 0
        rows[...] = jnp.concatenate([jnp.where(low, block, 0.0), jnp.where(low, 0.0, block)], 0).T

    def add(b, rows):
        for k in range(LANES):
            acc = accs[k % ACCS]
            at = pl.ds(row_ref[step, b, k], 1)
            acc[at, :] = acc[at, :] + rows[k:k + 1, :]

    turn(0, even)

    @pl.loop(0, BLK // 2)
    def _(i):
        turn(2 * i + 1, odd)
        add(2 * i, even)
        turn(jnp.minimum(2 * i + 2, BLK - 1), even)
        add(2 * i + 1, odd)

    @pl.loop(0, 9 * ROWS // 8, unroll=4)
    def _(i):
        part = pl.ds(pl.multiple_of(i * 8, 8), 8)
        total = accs[0][part, :]
        for acc in accs[1:]:
            total = total + acc[part, :]
        sums_ref[part, :] = total

    def note(slot, moved_by, where):
        order_ref[where] = slot
        pool_at[slot] = where + jnp.where(moved_by == 0, 0, BLK)

    place_slots(shift_ref, STEPS - 1, jnp.where(is_polar(), 4, 2), note)

    @pl.loop(0, BLK)
    def _(slot):
        source_ref[slot] = pool_at[arrival_ref[STEPS - 1, slot]]


def deposit(step, moved, cell_index, row, shift_list, arrival):
    sums, order, source = pl.pallas_call(
        functools.partial(deposit_kernel, step),
        out_shape=(
            jax.ShapeDtypeStruct((9 * ROWS, LANES), F32),
            jax.ShapeDtypeStruct((BLK,), jnp.int32),
            jax.ShapeDtypeStruct((BLK,), jnp.int32),
        ),
        in_specs=[VMEM, VMEM, SMEM, SMEM, SMEM],
        out_specs=(VMEM, SMEM, SMEM),
        scratch_shapes=[pltpu.VMEM((LANES, LANES), F32)] * 2
        + [pltpu.SMEM((BLK,), jnp.int32)]
        + [pltpu.VMEM((9 * ROWS, LANES), F32)] * ACCS,
        compiler_params=pltpu.CompilerParams(vmem_limit_bytes=LIMIT),
        name="deposit",
    )(moved, cell_index, row, shift_list, arrival)
    return sums.reshape(3, 3, ROWS, LANES), order, source


def split(x):
    high = x.astype(BF16)
    return high, (x - high.astype(F32)).astype(BF16)


def pairs_of(rates):
    zero = jnp.zeros((S, S), F32)
    high, low = split(jnp.concatenate([jnp.concatenate([rates, zero], 1), jnp.concatenate([zero, rates], 1)], 0))
    return jnp.concatenate([high, high], 1), low


def exchange_kernel(
    step, sums_ref, moved_ref, rates_ref, mix_ref, cell_ref, row_ref, order_ref, source_ref, out_ref,
    below, above, middle, left, right, table, chem, high2, low1, even, odd, reacted, pool,
    up_sem, down_sem, west_sem, east_sem, mwest_sem, meast_sem, mup_sem, mdown_sem, send_sem, recv_sem,
):
    last = step == STEPS - 1
    band = lax.axis_index("lat")
    bands = lax.axis_size("lat")
    has_up = band < bands - 1
    has_down = band > 0
    up = jnp.minimum(band + 1, bands - 1)
    down = jnp.maximum(band - 1, 0)
    east = around("lon", 1)
    west = around("lon", -1)
    beside = (1, -1) if last else (1, -1, 2, -2)
    barrier = pltpu.get_barrier_semaphore()
    for offset in beside:
        pl.semaphore_signal(barrier, inc=1, device_id={"lon": around("lon", offset)}, device_id_type=MESH)

    @pl.when(has_up)
    def _():
        pl.semaphore_signal(barrier, inc=1, device_id={"lat": up}, device_id_type=MESH)

    @pl.when(has_down)
    def _():
        pl.semaphore_signal(barrier, inc=1, device_id={"lat": down}, device_id_type=MESH)

    pl.semaphore_wait(barrier, len(beside) + has_up.astype(jnp.int32) + has_down.astype(jnp.int32))

    def remote(src, dst, sem, index, device):
        return pltpu.make_async_remote_copy(
            src_ref=src, dst_ref=dst, send_sem=sem.at[(0,) + index], recv_sem=sem.at[(1,) + index],
            device_id=device, device_id_type=MESH,
        )

    def chunk(c):
        return pl.ds(c * CHUNK, CHUNK)

    def sums_up(s, c):
        return remote(sums_ref.at[2, s, chunk(c)], below.at[s, chunk(c)], up_sem, (s, c), {"lat": up})

    def sums_down(s, c):
        return remote(sums_ref.at[0, s, chunk(c)], above.at[s, chunk(c)], down_sem, (s, c), {"lat": down})

    def sums_west(c):
        return remote(middle.at[0, chunk(c)], right.at[chunk(c)], west_sem, (c,), {"lon": west})

    def sums_east(c):
        return remote(middle.at[2, chunk(c)], left.at[chunk(c)], east_sem, (c,), {"lon": east})

    def means_west(c):
        return remote(table.at[1, 1, chunk(c)], table.at[1, 2, chunk(c)], mwest_sem, (c,), {"lon": west})

    def means_east(c):
        return remote(table.at[1, 1, chunk(c)], table.at[1, 0, chunk(c)], meast_sem, (c,), {"lon": east})

    def means_up(s, c):
        return remote(table.at[1, s, chunk(c)], table.at[0, s, chunk(c)], mup_sem, (s, c), {"lat": up})

    def means_down(s, c):
        return remote(table.at[1, s, chunk(c)], table.at[2, s, chunk(c)], mdown_sem, (s, c), {"lat": down})

    order = [(s, c) for c in LAST_FIRST for s in (0, 2, 1)]

    @pl.when(has_up)
    def _():
        for s, c in order:
            sums_up(s, c).start()

    @pl.when(has_down)
    def _():
        for s, c in order:
            sums_down(s, c).start()

    @pl.when(jnp.logical_not(has_down))
    def _():
        below[...] = jnp.zeros_like(below)
        table[0] = jnp.zeros_like(table[0])

    @pl.when(jnp.logical_not(has_up))
    def _():
        above[...] = jnp.zeros_like(above)
        table[2] = jnp.zeros_like(table[2])

    high, low = pairs_of(rates_ref[...])
    high2[...] = high
    low1[...] = low
    half_blk = BLK // 2
    for b in range(BLK):
        column = b % half_blk * LANES
        chem[b // half_blk, :, column:column + LANES] = moved_ref[b]

    def chemistry(substeps):
        def advance(_, current):
            state = chem[...].reshape(2 * S, half_blk * LANES)
            high, low = split(state)
            pushed = jnp.dot(high2[...], jnp.concatenate([high, low], 0), preferred_element_type=F32)
            pushed = pushed + jnp.dot(low1[...], high, preferred_element_type=F32)
            chem[...] = (state + (2.0 / SUB) * jnp.tanh(pushed)).reshape(2, S, half_blk * LANES)
            return current

        lax.fori_loop(0, substeps, advance, 0)

    def strips(body):
        @pl.loop(0, CHUNK // 8, unroll=4)
        def _(i):
            body(pl.multiple_of(i * 8, 8))

    lane = lax.broadcasted_iota(jnp.int32, (8, LANES), 1)
    spare = lane % 64 >= S

    def bands_summed(c):
        for s in (0, 2, 1):
            @pl.when(has_down)
            def _():
                sums_up(s, c).wait_recv()

            @pl.when(has_up)
            def _():
                sums_down(s, c).wait_recv()

            def add_bands(i):
                part = pl.ds(c * CHUNK + i, 8)
                middle[s, part, :] = sums_ref[1, s, part, :] + below[s, part, :] + above[s, part, :]

            strips(add_bands)
            if s == 0:
                sums_west(c).start()
            if s == 2:
                sums_east(c).start()

    def sectors_summed(c):
        sums_west(c).wait_recv()
        sums_east(c).wait_recv()

        def mean(i):
            part = pl.ds(c * CHUNK + i, 8)
            total = middle[1, part, :] + left[part, :] + right[part, :]
            count = jnp.where(lane < 64, total[:, S:S + 1], total[:, 64 + S:64 + S + 1])
            means = total / jnp.maximum(count, 1.0)
            if c < CHUNKS - 1:
                others = table[1, 1, pl.ds((CHUNKS - 1) * CHUNK + i, 8), :]
                means = jnp.where(spare, pltpu.roll(others, S - 16 * c, 1), means)
            table[1, 1, part, :] = means

        strips(mean)
        if c < CHUNKS - 1:
            means_west(c).start()
            means_east(c).start()

            @pl.when(has_up)
            def _():
                means_up(1, c).start()

            @pl.when(has_down)
            def _():
                means_down(1, c).start()

    def means_passed(c):
        means_west(c).wait_recv()
        means_east(c).wait_recv()

        @pl.when(has_up)
        def _():
            means_up(0, c).start()
            means_up(2, c).start()

        @pl.when(has_down)
        def _():
            means_down(0, c).start()
            means_down(2, c).start()

    parts = {"a": bands_summed, "b": sectors_summed, "c": means_passed}
    for entry in PLAN:
        if isinstance(entry, int):
            chemistry(entry)
        else:
            parts[entry[0]](entry[1])

    for b in range(BLK):
        column = b % half_blk * LANES
        reacted[b] = chem[b // half_blk, :, column:column + LANES]

    for s, c in order:
        @pl.when(has_up)
        def _():
            sums_up(s, c).wait_send()
            if c < CHUNKS - 1:
                means_up(s, c).wait_send()
                means_down(s, c).wait_recv()

        @pl.when(has_down)
        def _():
            sums_down(s, c).wait_send()
            if c < CHUNKS - 1:
                means_down(s, c).wait_send()
                means_up(s, c).wait_recv()
    for c in range(CHUNKS):
        sums_west(c).wait_send()
        sums_east(c).wait_send()
        if c < CHUNKS - 1:
            means_west(c).wait_send()
            means_east(c).wait_send()

    for r in range(3):
        for s in range(3):
            if (r, s) != (1, 1):
                def unpack(i):
                    found = [pltpu.roll(table[r, s, pl.ds(q * CHUNK + i, 8), :], LANES - S + 16 * q, 1) for q in range(3)]
                    spot = lane % 64
                    table[r, s, pl.ds(3 * CHUNK + i, 8), :] = jnp.where(spot < 16, found[0], jnp.where(spot < 32, found[1], found[2]))

                strips(unpack)

    mix = jnp.broadcast_to(mix_ref[...], (LANES, S)).T
    flat = table.reshape(9 * ROWS, LANES)

    def gather(b, rows):
        for k in range(LANES):
            rows[k:k + 1, :] = flat[pl.ds(row_ref[step, b, k], 1), :]

    def mixed(b, rows):
        means = rows[...].T
        low = (cell_ref[step, pl.ds(b, 1), :] & ROWS) == 0
        picked = jnp.where(low, means[0:S], means[64:64 + S])
        return reacted[b] + mix * (picked - moved_ref[b])

    def pair(order_of, target, i):
        first, second = order_of(2 * i), order_of(2 * i + 1)
        gather(first, even)
        gather(second, odd)
        target[2 * i] = mixed(first, even)
        target[2 * i + 1] = mixed(second, odd)

    if last:
        @pl.loop(0, BLK // 2)
        def _(i):
            pair(lambda b: b, out_ref, i)
    else:
        polar = is_polar()
        half_unit = jnp.where(polar, 2, 1)

        @pl.loop(0, 6)
        def _(k):
            @pl.loop(0, half_unit)
            def _(u):
                pair(lambda at: order_ref[at], pool, k * half_unit + u)

            for batch in range(6):
                @pl.when(k == batch)
                def _():
                    each_unit(polar, lambda unit: batch_copy(pool, send_sem, recv_sem, batch, unit).start())

        @pl.loop(6 * half_unit, BLK // 2)
        def _(i):
            pair(lambda at: order_ref[at], pool, i)

        def wait(unit):
            for k in range(6):
                batch_copy(pool, send_sem, recv_sem, k, unit).wait()

        each_unit(polar, wait)

        @pl.loop(0, BLK, unroll=4)
        def _(slot):
            out_ref[slot] = pool[source_ref[slot]]


def exchange(step, sums, moved, rates, mix, cell_index, row, order, source):
    region = (3, ROWS, LANES)
    pair = pltpu.SemaphoreType.DMA((2, 3, CHUNKS))
    single = pltpu.SemaphoreType.DMA((2, CHUNKS))
    return pl.pallas_call(
        functools.partial(exchange_kernel, step),
        out_shape=jax.ShapeDtypeStruct((BLK, S, LANES), F32),
        in_specs=[VMEM, VMEM, VMEM, VMEM, VMEM, SMEM, SMEM, SMEM],
        out_specs=VMEM,
        scratch_shapes=[
            pltpu.VMEM(region, F32),
            pltpu.VMEM(region, F32),
            pltpu.VMEM(region, F32),
            pltpu.VMEM((ROWS, LANES), F32),
            pltpu.VMEM((ROWS, LANES), F32),
            pltpu.VMEM((3, 3, ROWS, LANES), F32),
            pltpu.VMEM((2, S, BLK // 2 * LANES), F32),
            pltpu.VMEM((2 * S, 4 * S), BF16),
            pltpu.VMEM((2 * S, 2 * S), BF16),
            pltpu.VMEM((LANES, LANES), F32),
            pltpu.VMEM((LANES, LANES), F32),
            pltpu.VMEM((BLK, S, LANES), F32),
            pltpu.VMEM((2 * BLK, S, LANES), F32),
            pair, pair, single, single, single, single, pair, pair,
            pltpu.SemaphoreType.DMA((6,)),
            pltpu.SemaphoreType.DMA((6,)),
        ],
        compiler_params=pltpu.CompilerParams(collective_id=2 + step, has_side_effects=True, vmem_limit_bytes=LIMIT),
        name="exchange",
    )(sums, moved, rates, mix, cell_index, row, order, source)


def shards(species, reaction_rates, mix_rate, shift_list, arrival, cell_index):
    moved, row = migrate(shift_list, arrival, species, cell_index)
    mix = mix_rate.reshape(1, S)
    for step in range(STEPS):
        sums, order, source = deposit(step, moved, cell_index, row, shift_list, arrival)
        moved = exchange(step, sums, moved, reaction_rates, mix, cell_index, row, order, source)
    return moved


def solution(mesh):
    placed = (
        P(("lat", "lon"), None, None),
        P(),
        P(),
        P(None, "lat", None),
        P(None, ("lat", "lon")),
        P(None, ("lat", "lon"), None),
    )
    return jax.shard_map(
        shards, mesh=mesh, in_specs=placed, out_specs=P(("lat", "lon"), None, None), check_vma=False
    )
```

```python
import functools

import jax
import jax.numpy as jnp
from jax import lax
from jax.experimental import pallas as pl
from jax.experimental.pallas import tpu as pltpu
from jax.sharding import PartitionSpec as P

S = 48
LANES = 128
BLK = 32
CELL_DEV = 1024
ROWS = CELL_DEV // 2
STEPS = 2
SUB = 32
ACCS = 6
CHUNKS = 4
CHUNK = ROWS // CHUNKS
F32 = jnp.float32
BF16 = jnp.bfloat16
MESH = pl.DeviceIdType.MESH
VMEM = pl.BlockSpec(memory_space=pltpu.VMEM)
SMEM = pl.BlockSpec(memory_space=pltpu.SMEM)
HBM = pl.BlockSpec(memory_space=pltpu.HBM)
TABLE = jax.ShapeDtypeStruct((9 * ROWS, LANES), F32)
LIMIT = 24 * 2**20
BATCHES = (2, -2, 1, 1, -1, -1)
FIRST = {2: 0, -2: 1, 1: 2, -1: 4}
LAST_FIRST = (3, 0, 1, 2)
PLAN = (6, ("a", 3), 2, ("a", 0), 2, ("a", 1), 2, ("b", 3), ("a", 2), 3, ("b", 0), 2, ("b", 1), 2, ("b", 2), 3, ("c", 0), 3, ("c", 1), 3, ("c", 2), 4)


def around(axis, step):
    count = lax.axis_size(axis)
    return lax.rem(lax.axis_index(axis) + step + count, count)


def is_polar():
    band = lax.axis_index("lat")
    return (band == 0) | (band == lax.axis_size("lat") - 1)


def place_slots(shift_ref, step, unit, visit):
    def place(slot, counts):
        moved_by = shift_ref[step, 0, slot]
        where = 6 * unit + counts[4]
        later = []
        for offset, count in zip((2, -2, 1, -1), counts):
            hit = moved_by == offset
            where = jnp.where(hit, FIRST[offset] * unit + count, where)
            later.append(count + hit.astype(jnp.int32))
        later.append(counts[4] + (moved_by == 0).astype(jnp.int32))
        visit(slot, moved_by, jnp.minimum(where, BLK - 1))
        return tuple(later)

    lax.fori_loop(0, BLK, place, (jnp.int32(0),) * 5)


def batch_copy(pool, send_sem, recv_sem, k, unit):
    return pltpu.make_async_remote_copy(
        src_ref=pool.at[pl.ds(k * unit, unit)],
        dst_ref=pool.at[pl.ds(BLK + k * unit, unit)],
        send_sem=send_sem.at[k],
        recv_sem=recv_sem.at[k],
        device_id={"lon": around("lon", BATCHES[k])},
        device_id_type=MESH,
    )


def each_unit(polar, body):
    @pl.when(polar)
    def _():
        body(4)

    @pl.when(jnp.logical_not(polar))
    def _():
        body(2)


def blank_strips(refs):
    blank = jnp.zeros((8, LANES), F32)

    @pl.loop(0, 9 * ROWS // 8, unroll=4)
    def _(i):
        part = pl.ds(pl.multiple_of(i * 8, 8), 8)
        for ref in refs:
            ref[part, :] = blank


def migrate_kernel(shift_hbm, arrival_hbm, state_hbm, cell_hbm, moved_ref, row_ref, low_ref, place_ref, source_ref, *rest):
    accs = rest[:ACCS]
    shift_ref, arrival_ref, state_ref, cell_ref, pool, pool_at, load_sem, send_sem, recv_sem = rest[ACCS:]
    loads = [
        pltpu.make_async_copy(src, dst, load_sem.at[k])
        for k, (src, dst) in enumerate(
            ((shift_hbm, shift_ref), (arrival_hbm, arrival_ref), (state_hbm, state_ref), (cell_hbm, cell_ref))
        )
    ]
    for load in loads:
        load.start()
    polar = is_polar()
    unit = jnp.where(polar, 4, 2)
    barrier = pltpu.get_barrier_semaphore()
    for offset in (1, -1, 2, -2):
        pl.semaphore_signal(barrier, inc=1, device_id={"lon": around("lon", offset)}, device_id_type=MESH)

    def note(slot, moved_by, where):
        pool_at[slot] = where + jnp.where(moved_by == 0, 0, BLK)

    def note_later(slot, moved_by, where):
        place_ref[slot] = where + jnp.where(moved_by == 0, 0, BLK)

    loads[0].wait()
    place_slots(shift_ref, 0, unit, note)
    loads[1].wait()
    loads[2].wait()

    @pl.loop(0, 6 * unit)
    def _(where):
        def seek(slot, found):
            return jnp.where(pool_at[slot] == where + BLK, slot, found)

        pool[where] = state_ref[lax.fori_loop(0, BLK, seek, jnp.int32(0), unroll=True)]

    pl.semaphore_wait(barrier, 4)

    def start(unit):
        for k in range(6):
            batch_copy(pool, send_sem, recv_sem, k, unit).start()

    each_unit(polar, start)
    loads[3].wait()
    sectors = lax.axis_size("lon")
    cell = cell_ref[...]
    owner = cell // CELL_DEV
    rel_band = owner // sectors - lax.axis_index("lat") + 1
    rel_sector = (owner % sectors - lax.axis_index("lon") + 1 + sectors) % sectors
    row_ref[...] = jnp.clip((rel_band * 3 + rel_sector) * ROWS + cell % ROWS, 0, 9 * ROWS - 1)
    low_ref[...] = 1 - cell // ROWS % 2
    place_slots(shift_ref, STEPS - 1, unit, note_later)

    @pl.loop(0, BLK)
    def _(slot):
        source_ref[slot] = place_ref[arrival_ref[STEPS - 1, slot]]

    blank_strips(accs)

    def wait(unit):
        for k in range(6):
            batch_copy(pool, send_sem, recv_sem, k, unit).wait()

    each_unit(polar, wait)

    @pl.loop(0, BLK, unroll=4)
    def _(slot):
        old = arrival_ref[0, slot]
        at = pool_at[old]
        moved_ref[slot] = jnp.where(at < BLK, state_ref[old], pool[at])


def migrate(shift_list, arrival, state, cell_index):
    whole = jax.ShapeDtypeStruct((STEPS, BLK, LANES), jnp.int32)
    slots = jax.ShapeDtypeStruct((BLK,), jnp.int32)
    return pl.pallas_call(
        migrate_kernel,
        out_shape=(jax.ShapeDtypeStruct((BLK, S, LANES), F32), whole, whole, slots, slots) + (TABLE,) * ACCS,
        in_specs=[HBM] * 4,
        out_specs=(VMEM, VMEM, VMEM, SMEM, SMEM) + (VMEM,) * ACCS,
        scratch_shapes=[
            pltpu.SMEM((STEPS, 1, BLK), jnp.int32),
            pltpu.SMEM((STEPS, BLK), jnp.int32),
            pltpu.VMEM((BLK, S, LANES), F32),
            pltpu.VMEM((STEPS, BLK, LANES), jnp.int32),
            pltpu.VMEM((2 * BLK, S, LANES), F32),
            pltpu.SMEM((BLK,), jnp.int32),
            pltpu.SemaphoreType.DMA((4,)),
            pltpu.SemaphoreType.DMA((6,)),
            pltpu.SemaphoreType.DMA((6,)),
        ],
        compiler_params=pltpu.CompilerParams(collective_id=1, has_side_effects=True, vmem_limit_bytes=LIMIT),
        name="migrate",
    )(shift_list, arrival, state, cell_index)


def deposit_kernel(step, moved_ref, low_ref, row_ref, place_ref, *rest):
    accs = rest[ACCS:2 * ACCS]
    order_ref, even, odd = rest[2 * ACCS:]
    tail = jnp.where(lax.broadcasted_iota(jnp.int32, (16, LANES), 0) == 0, 1.0, 0.0)

    def turn(b, rows):
        block = jnp.concatenate([moved_ref[b], tail], 0)
        low = low_ref[step, pl.ds(b, 1), :] == 1
        rows[...] = jnp.concatenate([jnp.where(low, block, 0.0), jnp.where(low, 0.0, block)], 0).T

    def add(b, rows):
        for k in range(LANES):
            acc = accs[k % ACCS]
            at = pl.ds(row_ref[step, b, k], 1)
            acc[at, :] = acc[at, :] + rows[k:k + 1, :]

    turn(0, even)

    @pl.loop(0, BLK // 2)
    def _(i):
        turn(2 * i + 1, odd)
        add(2 * i, even)
        turn(jnp.minimum(2 * i + 2, BLK - 1), even)
        add(2 * i + 1, odd)

    @pl.loop(0, BLK)
    def _(slot):
        order_ref[place_ref[slot] % BLK] = slot


def deposit(step, moved, low, row, place, accs):
    *sums, order = pl.pallas_call(
        functools.partial(deposit_kernel, step),
        out_shape=(TABLE,) * ACCS + (jax.ShapeDtypeStruct((BLK,), jnp.int32),),
        in_specs=[VMEM, VMEM, SMEM, SMEM] + [VMEM] * ACCS,
        out_specs=(VMEM,) * ACCS + (SMEM,),
        input_output_aliases={4 + k: k for k in range(ACCS)},
        scratch_shapes=[pltpu.VMEM((LANES, LANES), F32)] * 2,
        compiler_params=pltpu.CompilerParams(vmem_limit_bytes=LIMIT),
        name="deposit",
    )(moved, low, row, place, *accs)
    return sums, order


def split(x):
    high = x.astype(BF16)
    return high, (x - high.astype(F32)).astype(BF16)


def pairs_of(rates):
    zero = jnp.zeros((S, S), F32)
    high, low = split(jnp.concatenate([jnp.concatenate([rates, zero], 1), jnp.concatenate([zero, rates], 1)], 0))
    return jnp.concatenate([high, high], 1), low


def exchange_kernel(
    step, moved_ref, rates_hbm, mix_hbm, low_ref, row_ref, order_ref, source_ref, *rest
):
    last = step == STEPS - 1
    accs = rest[:ACCS]
    out_ref = rest[ACCS]
    blanks = () if last else rest[ACCS + 1:2 * ACCS + 1]
    (
        sums_ref, rates_ref, mix_ref, below, above, middle, left, right, table, chem, high2, low1, even, odd, reacted, pool,
        up_sem, down_sem, west_sem, east_sem, mwest_sem, meast_sem, mup_sem, mdown_sem, send_sem, recv_sem, load_sem,
    ) = rest[ACCS + 1 + len(blanks):]
    loads = [
        pltpu.make_async_copy(rates_hbm, rates_ref, load_sem.at[0]),
        pltpu.make_async_copy(mix_hbm, mix_ref, load_sem.at[1]),
    ]
    for load in loads:
        load.start()

    def add_up(r):
        @pl.loop(0, 3 * ROWS // 8, unroll=4)
        def _(i):
            at = pl.multiple_of(i * 8, 8)
            part = pl.ds(r * 3 * ROWS + at, 8)
            total = accs[0][part, :]
            for acc in accs[1:]:
                total = total + acc[part, :]
            sums_ref[r, at // ROWS, pl.ds(pl.multiple_of(at % ROWS, 8), 8), :] = total

    band = lax.axis_index("lat")
    bands = lax.axis_size("lat")
    has_up = band < bands - 1
    has_down = band > 0
    up = jnp.minimum(band + 1, bands - 1)
    down = jnp.maximum(band - 1, 0)
    east = around("lon", 1)
    west = around("lon", -1)
    beside = (1, -1) if last else (1, -1, 2, -2)
    barrier = pltpu.get_barrier_semaphore()
    for offset in beside:
        pl.semaphore_signal(barrier, inc=1, device_id={"lon": around("lon", offset)}, device_id_type=MESH)

    @pl.when(has_up)
    def _():
        pl.semaphore_signal(barrier, inc=1, device_id={"lat": up}, device_id_type=MESH)

    @pl.when(has_down)
    def _():
        pl.semaphore_signal(barrier, inc=1, device_id={"lat": down}, device_id_type=MESH)

    add_up(2)
    add_up(0)
    pl.semaphore_wait(barrier, len(beside) + has_up.astype(jnp.int32) + has_down.astype(jnp.int32))

    def remote(src, dst, sem, index, device):
        return pltpu.make_async_remote_copy(
            src_ref=src, dst_ref=dst, send_sem=sem.at[(0,) + index], recv_sem=sem.at[(1,) + index],
            device_id=device, device_id_type=MESH,
        )

    def chunk(c):
        return pl.ds(c * CHUNK, CHUNK)

    def sums_up(s, c):
        return remote(sums_ref.at[2, s, chunk(c)], below.at[s, chunk(c)], up_sem, (s, c), {"lat": up})

    def sums_down(s, c):
        return remote(sums_ref.at[0, s, chunk(c)], above.at[s, chunk(c)], down_sem, (s, c), {"lat": down})

    def sums_west(c):
        return remote(middle.at[0, chunk(c)], right.at[chunk(c)], west_sem, (c,), {"lon": west})

    def sums_east(c):
        return remote(middle.at[2, chunk(c)], left.at[chunk(c)], east_sem, (c,), {"lon": east})

    def means_west(c):
        return remote(table.at[1, 1, chunk(c)], table.at[1, 2, chunk(c)], mwest_sem, (c,), {"lon": west})

    def means_east(c):
        return remote(table.at[1, 1, chunk(c)], table.at[1, 0, chunk(c)], meast_sem, (c,), {"lon": east})

    def means_up(s, c):
        return remote(table.at[1, s, chunk(c)], table.at[0, s, chunk(c)], mup_sem, (s, c), {"lat": up})

    def means_down(s, c):
        return remote(table.at[1, s, chunk(c)], table.at[2, s, chunk(c)], mdown_sem, (s, c), {"lat": down})

    order = [(s, c) for c in LAST_FIRST for s in (0, 2, 1)]

    @pl.when(has_up)
    def _():
        for s, c in order:
            sums_up(s, c).start()

    @pl.when(has_down)
    def _():
        for s, c in order:
            sums_down(s, c).start()

    @pl.when(jnp.logical_not(has_down))
    def _():
        below[...] = jnp.zeros_like(below)
        table[0] = jnp.zeros_like(table[0])

    @pl.when(jnp.logical_not(has_up))
    def _():
        above[...] = jnp.zeros_like(above)
        table[2] = jnp.zeros_like(table[2])

    add_up(1)
    for load in loads:
        load.wait()
    high, low = pairs_of(rates_ref[...])
    high2[...] = high
    low1[...] = low
    half_blk = BLK // 2
    for b in range(BLK):
        column = b % half_blk * LANES
        chem[b // half_blk, :, column:column + LANES] = moved_ref[b]

    def chemistry(substeps):
        def advance(_, current):
            state = chem[...].reshape(2 * S, half_blk * LANES)
            high, low = split(state)
            pushed = jnp.dot(high2[...], jnp.concatenate([high, low], 0), preferred_element_type=F32)
            pushed = pushed + jnp.dot(low1[...], high, preferred_element_type=F32)
            chem[...] = (state + (2.0 / SUB) * jnp.tanh(pushed)).reshape(2, S, half_blk * LANES)
            return current

        lax.fori_loop(0, substeps, advance, 0)

    def strips(body):
        @pl.loop(0, CHUNK // 8, unroll=4)
        def _(i):
            body(pl.multiple_of(i * 8, 8))

    lane = lax.broadcasted_iota(jnp.int32, (8, LANES), 1)
    spare = lane % 64 >= S

    def bands_summed(c):
        for s in (0, 2, 1):
            @pl.when(has_down)
            def _():
                sums_up(s, c).wait_recv()

            @pl.when(has_up)
            def _():
                sums_down(s, c).wait_recv()

            def add_bands(i):
                part = pl.ds(c * CHUNK + i, 8)
                middle[s, part, :] = sums_ref[1, s, part, :] + below[s, part, :] + above[s, part, :]

            strips(add_bands)
            if s == 0:
                sums_west(c).start()
            if s == 2:
                sums_east(c).start()

    def sectors_summed(c):
        sums_west(c).wait_recv()
        sums_east(c).wait_recv()

        def mean(i):
            part = pl.ds(c * CHUNK + i, 8)
            total = middle[1, part, :] + left[part, :] + right[part, :]
            count = jnp.where(lane < 64, total[:, S:S + 1], total[:, 64 + S:64 + S + 1])
            means = total / jnp.maximum(count, 1.0)
            if c < CHUNKS - 1:
                others = table[1, 1, pl.ds((CHUNKS - 1) * CHUNK + i, 8), :]
                means = jnp.where(spare, pltpu.roll(others, S - 16 * c, 1), means)
            table[1, 1, part, :] = means

        strips(mean)
        if c < CHUNKS - 1:
            means_west(c).start()
            means_east(c).start()

            @pl.when(has_up)
            def _():
                means_up(1, c).start()

            @pl.when(has_down)
            def _():
                means_down(1, c).start()

    def means_passed(c):
        means_west(c).wait_recv()
        means_east(c).wait_recv()

        @pl.when(has_up)
        def _():
            means_up(0, c).start()
            means_up(2, c).start()

        @pl.when(has_down)
        def _():
            means_down(0, c).start()
            means_down(2, c).start()

    parts = {"a": bands_summed, "b": sectors_summed, "c": means_passed}
    for entry in PLAN:
        if isinstance(entry, int):
            chemistry(entry)
        else:
            parts[entry[0]](entry[1])

    if not last:
        blank_strips(blanks)
    for b in range(BLK):
        column = b % half_blk * LANES
        reacted[b] = chem[b // half_blk, :, column:column + LANES]

    for s, c in order:
        @pl.when(has_up)
        def _():
            sums_up(s, c).wait_send()
            if c < CHUNKS - 1:
                means_up(s, c).wait_send()
                means_down(s, c).wait_recv()

        @pl.when(has_down)
        def _():
            sums_down(s, c).wait_send()
            if c < CHUNKS - 1:
                means_down(s, c).wait_send()
                means_up(s, c).wait_recv()
    for c in range(CHUNKS):
        sums_west(c).wait_send()
        sums_east(c).wait_send()
        if c < CHUNKS - 1:
            means_west(c).wait_send()
            means_east(c).wait_send()

    for r in range(3):
        for s in range(3):
            if (r, s) != (1, 1):
                def unpack(i):
                    found = [pltpu.roll(table[r, s, pl.ds(q * CHUNK + i, 8), :], LANES - S + 16 * q, 1) for q in range(3)]
                    spot = lane % 64
                    table[r, s, pl.ds(3 * CHUNK + i, 8), :] = jnp.where(spot < 16, found[0], jnp.where(spot < 32, found[1], found[2]))

                strips(unpack)

    mix = jnp.broadcast_to(mix_ref[...], (LANES, S)).T
    flat = table.reshape(9 * ROWS, LANES)

    def gather(b, rows):
        for k in range(LANES):
            rows[k:k + 1, :] = flat[pl.ds(row_ref[step, b, k], 1), :]

    def mixed(b, rows):
        means = rows[...].T
        low = low_ref[step, pl.ds(b, 1), :] == 1
        picked = jnp.where(low, means[0:S], means[64:64 + S])
        return reacted[b] + mix * (picked - moved_ref[b])

    def pair(order_of, target, i):
        first, second = order_of(2 * i), order_of(2 * i + 1)
        gather(first, even)
        gather(second, odd)
        target[2 * i] = mixed(first, even)
        target[2 * i + 1] = mixed(second, odd)

    if last:
        @pl.loop(0, BLK // 2)
        def _(i):
            pair(lambda b: b, out_ref, i)
    else:
        polar = is_polar()
        half_unit = jnp.where(polar, 2, 1)

        @pl.loop(0, 6)
        def _(k):
            @pl.loop(0, half_unit)
            def _(u):
                pair(lambda at: order_ref[at], pool, k * half_unit + u)

            for batch in range(6):
                @pl.when(k == batch)
                def _():
                    each_unit(polar, lambda unit: batch_copy(pool, send_sem, recv_sem, batch, unit).start())

        @pl.loop(6 * half_unit, BLK // 2)
        def _(i):
            pair(lambda at: order_ref[at], pool, i)

        def wait(unit):
            for k in range(6):
                batch_copy(pool, send_sem, recv_sem, k, unit).wait()

        each_unit(polar, wait)

        @pl.loop(0, BLK, unroll=4)
        def _(slot):
            out_ref[slot] = pool[source_ref[slot]]


def exchange(step, sums, moved, rates, mix, low, row, order, source):
    region = (3, ROWS, LANES)
    pair = pltpu.SemaphoreType.DMA((2, 3, CHUNKS))
    single = pltpu.SemaphoreType.DMA((2, CHUNKS))
    blanks = 0 if step == STEPS - 1 else ACCS
    state = jax.ShapeDtypeStruct((BLK, S, LANES), F32)
    return pl.pallas_call(
        functools.partial(exchange_kernel, step),
        out_shape=(state,) + (TABLE,) * blanks,
        in_specs=[VMEM, HBM, HBM, VMEM, SMEM, SMEM, SMEM] + [VMEM] * ACCS,
        out_specs=(VMEM,) * (1 + blanks),
        scratch_shapes=[
            pltpu.VMEM((3, 3, ROWS, LANES), F32),
            pltpu.VMEM((S, S), F32),
            pltpu.VMEM((1, S), F32),
            pltpu.VMEM(region, F32),
            pltpu.VMEM(region, F32),
            pltpu.VMEM(region, F32),
            pltpu.VMEM((ROWS, LANES), F32),
            pltpu.VMEM((ROWS, LANES), F32),
            pltpu.VMEM((3, 3, ROWS, LANES), F32),
            pltpu.VMEM((2, S, BLK // 2 * LANES), F32),
            pltpu.VMEM((2 * S, 4 * S), BF16),
            pltpu.VMEM((2 * S, 2 * S), BF16),
            pltpu.VMEM((LANES, LANES), F32),
            pltpu.VMEM((LANES, LANES), F32),
            pltpu.VMEM((BLK, S, LANES), F32),
            pltpu.VMEM((2 * BLK, S, LANES), F32),
            pair, pair, single, single, single, single, pair, pair,
            pltpu.SemaphoreType.DMA((6,)),
            pltpu.SemaphoreType.DMA((6,)),
            pltpu.SemaphoreType.DMA((2,)),
        ],
        compiler_params=pltpu.CompilerParams(collective_id=2 + step, has_side_effects=True, vmem_limit_bytes=LIMIT),
        name="exchange",
    )(moved, rates, mix, low, row, order, source, *sums)


def shards(species, reaction_rates, mix_rate, shift_list, arrival, cell_index):
    inputs = (pltpu.with_memory_space_constraint(x, pltpu.HBM) for x in (shift_list, arrival, species, cell_index))
    moved, row, low, place, source, *accs = migrate(*inputs)
    mix = mix_rate.reshape(1, S)
    for step in range(STEPS):
        sums, order = deposit(step, moved, low, row, place, accs)
        moved, *accs = exchange(step, sums, moved, reaction_rates, mix, low, row, order, source)
    return moved


def solution(mesh):
    placed = (
        P(("lat", "lon"), None, None),
        P(),
        P(),
        P(None, "lat", None),
        P(None, ("lat", "lon")),
        P(None, ("lat", "lon"), None),
    )
    return jax.shard_map(
        shards, mesh=mesh, in_specs=placed, out_specs=P(("lat", "lon"), None, None), check_vma=False
    )
```

```python
import functools

import jax
import jax.numpy as jnp
from jax import lax
from jax.experimental import pallas as pl
from jax.experimental.pallas import tpu as pltpu
from jax.sharding import PartitionSpec as P

S = 48
LANES = 128
BLK = 32
CELL_DEV = 1024
ROWS = CELL_DEV // 2
STEPS = 2
SUB = 32
ACCS = 6
QUARTER = ROWS // 4
PACKED = 3 * QUARTER
PIECES = 6
PIECE = PACKED // PIECES
F32 = jnp.float32
BF16 = jnp.bfloat16
MESH = pl.DeviceIdType.MESH
VMEM = pl.BlockSpec(memory_space=pltpu.VMEM)
SMEM = pl.BlockSpec(memory_space=pltpu.SMEM)
HBM = pl.BlockSpec(memory_space=pltpu.HBM)
TABLE = jax.ShapeDtypeStruct((9 * ROWS, LANES), F32)
LIMIT = 24 * 2**20
BATCHES = (2, -2, 1, 1, -1, -1)
FIRST = {2: 0, -2: 1, 1: 2, -1: 4}
PLAN = (
    ("a", 0), 1, ("a", 1), 1, ("a", 2), 2, ("a", 3), 1, ("a", 4), 1, ("a", 5), 1,
    ("o", 0), ("b", 0), 1, ("o", 1), ("b", 1), 1, ("o", 2), ("b", 2), 1, ("o", 3), ("b", 3), 1, ("o", 4), ("b", 4), 1, ("o", 5), ("b", 5),
    2, ("c", 0), 2, ("c", 1), 2, ("c", 2), 2, ("c", 3), 2, ("c", 4), 2, ("c", 5), 3,
)
EARLY = 5


def around(axis, step):
    count = lax.axis_size(axis)
    return lax.rem(lax.axis_index(axis) + step + count, count)


def is_polar():
    band = lax.axis_index("lat")
    return (band == 0) | (band == lax.axis_size("lat") - 1)


def place_slots(shift_ref, step, unit, visit):
    def place(slot, counts):
        moved_by = shift_ref[step, 0, slot]
        where = 6 * unit + counts[4]
        later = []
        for offset, count in zip((2, -2, 1, -1), counts):
            hit = moved_by == offset
            where = jnp.where(hit, FIRST[offset] * unit + count, where)
            later.append(count + hit.astype(jnp.int32))
        later.append(counts[4] + (moved_by == 0).astype(jnp.int32))
        visit(slot, moved_by, jnp.minimum(where, BLK - 1))
        return tuple(later)

    lax.fori_loop(0, BLK, place, (jnp.int32(0),) * 5)


def batch_copy(pool, send_sem, recv_sem, k, unit):
    return pltpu.make_async_remote_copy(
        src_ref=pool.at[pl.ds(k * unit, unit)],
        dst_ref=pool.at[pl.ds(BLK + k * unit, unit)],
        send_sem=send_sem.at[k],
        recv_sem=recv_sem.at[k],
        device_id={"lon": around("lon", BATCHES[k])},
        device_id_type=MESH,
    )


def each_unit(polar, body):
    @pl.when(polar)
    def _():
        body(4)

    @pl.when(jnp.logical_not(polar))
    def _():
        body(2)


def blank_strips(refs):
    blank = jnp.zeros((8, LANES), F32)

    @pl.loop(0, 9 * ROWS // 8, unroll=4)
    def _(i):
        part = pl.ds(pl.multiple_of(i * 8, 8), 8)
        for ref in refs:
            ref[part, :] = blank


def migrate_kernel(shift_hbm, arrival_hbm, state_hbm, cell_hbm, moved_ref, row_ref, low_ref, place_ref, source_ref, *rest):
    accs = rest[:ACCS]
    shift_ref, arrival_ref, state_ref, cell_ref, pool, pool_at, load_sem, send_sem, recv_sem = rest[ACCS:]
    loads = [
        pltpu.make_async_copy(src, dst, load_sem.at[k])
        for k, (src, dst) in enumerate(
            ((shift_hbm, shift_ref), (arrival_hbm, arrival_ref), (state_hbm, state_ref), (cell_hbm, cell_ref))
        )
    ]
    for load in loads:
        load.start()
    polar = is_polar()
    unit = jnp.where(polar, 4, 2)
    barrier = pltpu.get_barrier_semaphore()
    for offset in (1, -1, 2, -2):
        pl.semaphore_signal(barrier, inc=1, device_id={"lon": around("lon", offset)}, device_id_type=MESH)

    def note(slot, moved_by, where):
        pool_at[slot] = where + jnp.where(moved_by == 0, 0, BLK)

    def note_later(slot, moved_by, where):
        place_ref[slot] = where + jnp.where(moved_by == 0, 0, BLK)

    loads[0].wait()
    place_slots(shift_ref, 0, unit, note)
    loads[1].wait()
    loads[2].wait()

    @pl.loop(0, 6 * unit)
    def _(where):
        def seek(slot, found):
            return jnp.where(pool_at[slot] == where + BLK, slot, found)

        pool[where] = state_ref[lax.fori_loop(0, BLK, seek, jnp.int32(0), unroll=True)]

    pl.semaphore_wait(barrier, 4)

    def start(unit):
        for k in range(6):
            batch_copy(pool, send_sem, recv_sem, k, unit).start()

    each_unit(polar, start)
    loads[3].wait()
    sectors = lax.axis_size("lon")
    cell = cell_ref[...]
    owner = cell // CELL_DEV
    rel_band = owner // sectors - lax.axis_index("lat") + 1
    rel_sector = (owner % sectors - lax.axis_index("lon") + 1 + sectors) % sectors
    row_ref[...] = jnp.clip((rel_band * 3 + rel_sector) * ROWS + cell % ROWS, 0, 9 * ROWS - 1)
    low_ref[...] = 1 - cell // ROWS % 2
    place_slots(shift_ref, STEPS - 1, unit, note_later)

    @pl.loop(0, BLK)
    def _(slot):
        source_ref[slot] = place_ref[arrival_ref[STEPS - 1, slot]]

    blank_strips(accs)

    def wait(unit):
        for k in range(6):
            batch_copy(pool, send_sem, recv_sem, k, unit).wait()

    each_unit(polar, wait)

    @pl.loop(0, BLK, unroll=4)
    def _(slot):
        old = arrival_ref[0, slot]
        at = pool_at[old]
        moved_ref[slot] = jnp.where(at < BLK, state_ref[old], pool[at])


def migrate(shift_list, arrival, state, cell_index):
    whole = jax.ShapeDtypeStruct((STEPS, BLK, LANES), jnp.int32)
    slots = jax.ShapeDtypeStruct((BLK,), jnp.int32)
    return pl.pallas_call(
        migrate_kernel,
        out_shape=(jax.ShapeDtypeStruct((BLK, S, LANES), F32), whole, whole, slots, slots) + (TABLE,) * ACCS,
        in_specs=[HBM] * 4,
        out_specs=(VMEM, VMEM, VMEM, SMEM, SMEM) + (VMEM,) * ACCS,
        scratch_shapes=[
            pltpu.SMEM((STEPS, 1, BLK), jnp.int32),
            pltpu.SMEM((STEPS, BLK), jnp.int32),
            pltpu.VMEM((BLK, S, LANES), F32),
            pltpu.VMEM((STEPS, BLK, LANES), jnp.int32),
            pltpu.VMEM((2 * BLK, S, LANES), F32),
            pltpu.SMEM((BLK,), jnp.int32),
            pltpu.SemaphoreType.DMA((4,)),
            pltpu.SemaphoreType.DMA((6,)),
            pltpu.SemaphoreType.DMA((6,)),
        ],
        compiler_params=pltpu.CompilerParams(collective_id=1, has_side_effects=True, vmem_limit_bytes=LIMIT),
        name="migrate",
    )(shift_list, arrival, state, cell_index)


def deposit_kernel(step, moved_ref, low_ref, row_ref, place_ref, *rest):
    accs = rest[ACCS:2 * ACCS]
    order_ref, even, odd = rest[2 * ACCS:]
    tail = jnp.where(lax.broadcasted_iota(jnp.int32, (16, LANES), 0) == 0, 1.0, 0.0)

    def turn(b, rows):
        block = jnp.concatenate([moved_ref[b], tail], 0)
        low = low_ref[step, pl.ds(b, 1), :] == 1
        rows[...] = jnp.concatenate([jnp.where(low, block, 0.0), jnp.where(low, 0.0, block)], 0).T

    def add(b, rows):
        for k in range(LANES):
            acc = accs[k % ACCS]
            at = pl.ds(row_ref[step, b, k], 1)
            acc[at, :] = acc[at, :] + rows[k:k + 1, :]

    turn(0, even)

    @pl.loop(0, BLK // 2)
    def _(i):
        turn(2 * i + 1, odd)
        add(2 * i, even)
        turn(jnp.minimum(2 * i + 2, BLK - 1), even)
        add(2 * i + 1, odd)

    @pl.loop(0, BLK)
    def _(slot):
        order_ref[place_ref[slot] % BLK] = slot


def deposit(step, moved, low, row, place, accs):
    *sums, order = pl.pallas_call(
        functools.partial(deposit_kernel, step),
        out_shape=(TABLE,) * ACCS + (jax.ShapeDtypeStruct((BLK,), jnp.int32),),
        in_specs=[VMEM, VMEM, SMEM, SMEM] + [VMEM] * ACCS,
        out_specs=(VMEM,) * ACCS + (SMEM,),
        input_output_aliases={4 + k: k for k in range(ACCS)},
        scratch_shapes=[pltpu.VMEM((LANES, LANES), F32)] * 2,
        compiler_params=pltpu.CompilerParams(vmem_limit_bytes=LIMIT),
        name="deposit",
    )(moved, low, row, place, *accs)
    return sums, order


def split(x):
    high = x.astype(BF16)
    return high, (x - high.astype(F32)).astype(BF16)


def pairs_of(rates):
    zero = jnp.zeros((S, S), F32)
    high, low = split(jnp.concatenate([jnp.concatenate([rates, zero], 1), jnp.concatenate([zero, rates], 1)], 0))
    return jnp.concatenate([high, high], 1), low


def exchange_kernel(
    step, moved_ref, rates_hbm, mix_hbm, low_ref, row_ref, order_ref, source_ref, *rest
):
    last = step == STEPS - 1
    accs = rest[:ACCS]
    out_ref = rest[ACCS]
    blanks = () if last else rest[ACCS + 1:2 * ACCS + 1]
    (
        sums_ref, counts, tallies, rates_ref, mix_ref, below, above, tally_below, tally_above, middle, tally_middle,
        left, right, tally_left, tally_right, factors, table, chem, high2, low1, even, odd, reacted, pool,
        up_sem, down_sem, west_sem, east_sem, mwest_sem, meast_sem, mup_sem, mdown_sem, tally_sem, send_sem, recv_sem, load_sem,
    ) = rest[ACCS + 1 + len(blanks):]
    loads = [
        pltpu.make_async_copy(rates_hbm, rates_ref, load_sem.at[0]),
        pltpu.make_async_copy(mix_hbm, mix_ref, load_sem.at[1]),
    ]
    lane = lax.broadcasted_iota(jnp.int32, (8, LANES), 1)
    spot = lane % 64
    spare = spot >= S
    for load in loads:
        load.start()

    def add_up(r):
        @pl.loop(0, QUARTER // 8)
        def _(i):
            at = pl.multiple_of(i * 8, 8)
            tally = jnp.zeros((8, LANES), F32)
            for s in range(3):
                quarters = []
                for q in range(4):
                    part = pl.ds((r * 3 + s) * ROWS + q * QUARTER + at, 8)
                    total = accs[0][part, :]
                    for acc in accs[1:]:
                        total = total + acc[part, :]
                    quarters.append(total)
                    tally = jnp.where(spot == s * 8 + q, pltpu.roll(total, (s * 8 + q - S) % LANES, 1), tally)
                for q in range(3):
                    sums_ref[r, s, pl.ds(q * QUARTER + at, 8), :] = jnp.where(
                        spare, pltpu.roll(quarters[3], S - 16 * q, 1), quarters[q]
                    )
            counts[pl.ds(at, 8), :] = tally

        tallies[r] = counts[...].T.reshape(2, 64, LANES)

    band = lax.axis_index("lat")
    bands = lax.axis_size("lat")
    has_up = band < bands - 1
    has_down = band > 0
    up = jnp.minimum(band + 1, bands - 1)
    down = jnp.maximum(band - 1, 0)
    east = around("lon", 1)
    west = around("lon", -1)
    beside = (1, -1) if last else (1, -1, 2, -2)
    barrier = pltpu.get_barrier_semaphore()
    for offset in beside:
        pl.semaphore_signal(barrier, inc=1, device_id={"lon": around("lon", offset)}, device_id_type=MESH)

    @pl.when(has_up)
    def _():
        pl.semaphore_signal(barrier, inc=1, device_id={"lat": up}, device_id_type=MESH)

    @pl.when(has_down)
    def _():
        pl.semaphore_signal(barrier, inc=1, device_id={"lat": down}, device_id_type=MESH)

    add_up(2)
    add_up(0)
    pl.semaphore_wait(barrier, len(beside) + has_up.astype(jnp.int32) + has_down.astype(jnp.int32))

    def remote(src, dst, sem, index, device):
        return pltpu.make_async_remote_copy(
            src_ref=src, dst_ref=dst, send_sem=sem.at[(0,) + index], recv_sem=sem.at[(1,) + index],
            device_id=device, device_id_type=MESH,
        )

    def piece(p):
        return pl.ds(p * PIECE, PIECE)

    def sums_up(s, p):
        return remote(sums_ref.at[2, s, piece(p)], below.at[s, piece(p)], up_sem, (s, p), {"lat": up})

    def sums_down(s, p):
        return remote(sums_ref.at[0, s, piece(p)], above.at[s, piece(p)], down_sem, (s, p), {"lat": down})

    def sums_west(p):
        return remote(middle.at[0, piece(p)], right.at[piece(p)], west_sem, (p,), {"lon": west})

    def sums_east(p):
        return remote(middle.at[2, piece(p)], left.at[piece(p)], east_sem, (p,), {"lon": east})

    def means_west(p):
        return remote(table.at[1, 1, piece(p)], table.at[1, 2, piece(p)], mwest_sem, (p,), {"lon": west})

    def means_east(p):
        return remote(table.at[1, 1, piece(p)], table.at[1, 0, piece(p)], meast_sem, (p,), {"lon": east})

    def means_up(s, p):
        return remote(table.at[1, s, piece(p)], table.at[0, s, piece(p)], mup_sem, (s, p), {"lat": up})

    def means_down(s, p):
        return remote(table.at[1, s, piece(p)], table.at[2, s, piece(p)], mdown_sem, (s, p), {"lat": down})

    def tally_up():
        return remote(tallies.at[2, :, pl.ds(0, 24)], tally_below, tally_sem, (0,), {"lat": up})

    def tally_down():
        return remote(tallies.at[0, :, pl.ds(0, 24)], tally_above, tally_sem, (1,), {"lat": down})

    def tally_west():
        return remote(tally_middle.at[:, pl.ds(0, 8)], tally_right, tally_sem, (2,), {"lon": west})

    def tally_east():
        return remote(tally_middle.at[:, pl.ds(16, 8)], tally_left, tally_sem, (3,), {"lon": east})

    order = [(s, p) for p in range(PIECES) for s in (0, 2)] + [(1, p) for p in range(PIECES)]

    @pl.when(has_up)
    def _():
        tally_up().start()
        for s, p in order:
            sums_up(s, p).start()

    @pl.when(has_down)
    def _():
        tally_down().start()
        for s, p in order:
            sums_down(s, p).start()

    @pl.when(jnp.logical_not(has_down))
    def _():
        below[...] = jnp.zeros_like(below)
        tally_below[...] = jnp.zeros_like(tally_below)
        table[0] = jnp.zeros_like(table[0])

    @pl.when(jnp.logical_not(has_up))
    def _():
        above[...] = jnp.zeros_like(above)
        tally_above[...] = jnp.zeros_like(tally_above)
        table[2] = jnp.zeros_like(table[2])

    add_up(1)
    for load in loads:
        load.wait()
    high, low = pairs_of(rates_ref[...])
    high2[...] = high
    low1[...] = low
    half_blk = BLK // 2
    for b in range(BLK):
        column = b % half_blk * LANES
        chem[b // half_blk, :, column:column + LANES] = moved_ref[b]

    def chemistry(substeps):
        def advance(_, current):
            state = chem[...].reshape(2 * S, half_blk * LANES)
            high, low = split(state)
            pushed = jnp.dot(high2[...], jnp.concatenate([high, low], 0), preferred_element_type=F32)
            pushed = pushed + jnp.dot(low1[...], high, preferred_element_type=F32)
            chem[...] = (state + (2.0 / SUB) * jnp.tanh(pushed)).reshape(2, S, half_blk * LANES)
            return current

        lax.fori_loop(0, substeps, advance, 0)

    chemistry(EARLY)

    def strips(first, rows, body):
        @pl.loop(0, rows // 8, unroll=4)
        def _(i):
            body(pl.multiple_of(i * 8, 8) + first)

    def bands_summed(s, p):
        @pl.when(has_down)
        def _():
            sums_up(s, p).wait_recv()

        @pl.when(has_up)
        def _():
            sums_down(s, p).wait_recv()

        def add_bands(i):
            part = pl.ds(i, 8)
            middle[s, part, :] = sums_ref[1, s, part, :] + below[s, part, :] + above[s, part, :]

        strips(p * PIECE, PIECE, add_bands)

    def sides_summed(p):
        if p == 0:
            @pl.when(has_down)
            def _():
                tally_up().wait_recv()

            @pl.when(has_up)
            def _():
                tally_down().wait_recv()

            tally_middle[...] = tallies[1, :, 0:24] + tally_below[...] + tally_above[...]
            tally_west().start()
            tally_east().start()
        bands_summed(0, p)
        sums_west(p).start()
        bands_summed(2, p)
        sums_east(p).start()

    def own_summed(p):
        bands_summed(1, p)

    def sectors_summed(p):
        if p == 0:
            tally_west().wait_recv()
            tally_east().wait_recv()
            tally = tally_middle[:, 8:16] + tally_left[...] + tally_right[...]
            inverse = (1.0 / jnp.maximum(tally, 1.0)).reshape(16, LANES)
            factors[...] = jnp.concatenate([inverse, jnp.zeros((LANES - 16, LANES), F32)], 0).T
        sums_west(p).wait_recv()
        sums_east(p).wait_recv()
        q = p * PIECE // QUARTER

        def mean(i):
            part = pl.ds(i, 8)
            factor = factors[pl.ds(i - q * QUARTER, 8), :]
            low = jnp.where(spare, factor[:, 3:4], factor[:, q:q + 1])
            high = jnp.where(spare, factor[:, 11:12], factor[:, 8 + q:9 + q])
            total = middle[1, part, :] + left[part, :] + right[part, :]
            table[1, 1, part, :] = total * jnp.where(lane < 64, low, high)

        strips(p * PIECE, PIECE, mean)
        means_west(p).start()
        means_east(p).start()

        @pl.when(has_up)
        def _():
            means_up(1, p).start()

        @pl.when(has_down)
        def _():
            means_down(1, p).start()

    def means_passed(p):
        means_west(p).wait_recv()
        means_east(p).wait_recv()

        @pl.when(has_up)
        def _():
            means_up(0, p).start()
            means_up(2, p).start()

        @pl.when(has_down)
        def _():
            means_down(0, p).start()
            means_down(2, p).start()

    parts = {"a": sides_summed, "o": own_summed, "b": sectors_summed, "c": means_passed}
    for entry in PLAN:
        if isinstance(entry, int):
            chemistry(entry)
        else:
            parts[entry[0]](entry[1])

    if not last:
        blank_strips(blanks)
    for b in range(BLK):
        column = b % half_blk * LANES
        reacted[b] = chem[b // half_blk, :, column:column + LANES]

    @pl.when(has_up)
    def _():
        tally_up().wait_send()
        for s, p in order:
            sums_up(s, p).wait_send()
            means_up(s, p).wait_send()
            means_down(s, p).wait_recv()

    @pl.when(has_down)
    def _():
        tally_down().wait_send()
        for s, p in order:
            sums_down(s, p).wait_send()
            means_down(s, p).wait_send()
            means_up(s, p).wait_recv()

    tally_west().wait_send()
    tally_east().wait_send()
    for p in range(PIECES):
        for copy in (sums_west(p), sums_east(p), means_west(p), means_east(p)):
            copy.wait_send()

    for r in range(3):
        for s in range(3):
            def unpack(i):
                found = [pltpu.roll(table[r, s, pl.ds(q * QUARTER + i, 8), :], LANES - S + 16 * q, 1) for q in range(3)]
                table[r, s, pl.ds(PACKED + i, 8), :] = jnp.where(spot < 16, found[0], jnp.where(spot < 32, found[1], found[2]))

            strips(0, QUARTER, unpack)

    mix = jnp.broadcast_to(mix_ref[...], (LANES, S)).T
    flat = table.reshape(9 * ROWS, LANES)

    def gather(b, rows):
        for k in range(LANES):
            rows[k:k + 1, :] = flat[pl.ds(row_ref[step, b, k], 1), :]

    def mixed(b, rows):
        means = rows[...].T
        low = low_ref[step, pl.ds(b, 1), :] == 1
        picked = jnp.where(low, means[0:S], means[64:64 + S])
        return reacted[b] + mix * (picked - moved_ref[b])

    def pair(order_of, target, i):
        first, second = order_of(2 * i), order_of(2 * i + 1)
        gather(first, even)
        gather(second, odd)
        target[2 * i] = mixed(first, even)
        target[2 * i + 1] = mixed(second, odd)

    if last:
        @pl.loop(0, BLK // 2)
        def _(i):
            pair(lambda b: b, out_ref, i)
    else:
        polar = is_polar()
        half_unit = jnp.where(polar, 2, 1)

        @pl.loop(0, 6)
        def _(k):
            @pl.loop(0, half_unit)
            def _(u):
                pair(lambda at: order_ref[at], pool, k * half_unit + u)

            for batch in range(6):
                @pl.when(k == batch)
                def _():
                    each_unit(polar, lambda unit: batch_copy(pool, send_sem, recv_sem, batch, unit).start())

        @pl.loop(6 * half_unit, BLK // 2)
        def _(i):
            pair(lambda at: order_ref[at], pool, i)

        def wait(unit):
            for k in range(6):
                batch_copy(pool, send_sem, recv_sem, k, unit).wait()

        each_unit(polar, wait)

        @pl.loop(0, BLK, unroll=4)
        def _(slot):
            out_ref[slot] = pool[source_ref[slot]]


def exchange(step, sums, moved, rates, mix, low, row, order, source):
    region = pltpu.VMEM((3, PACKED, LANES), F32)
    beside = pltpu.VMEM((PACKED, LANES), F32)
    tally = pltpu.VMEM((2, 24, LANES), F32)
    tally_beside = pltpu.VMEM((2, 8, LANES), F32)
    square = pltpu.VMEM((LANES, LANES), F32)
    pair = pltpu.SemaphoreType.DMA((2, 3, PIECES))
    single = pltpu.SemaphoreType.DMA((2, PIECES))
    blanks = 0 if step == STEPS - 1 else ACCS
    state = jax.ShapeDtypeStruct((BLK, S, LANES), F32)
    return pl.pallas_call(
        functools.partial(exchange_kernel, step),
        out_shape=(state,) + (TABLE,) * blanks,
        in_specs=[VMEM, HBM, HBM, VMEM, SMEM, SMEM, SMEM] + [VMEM] * ACCS,
        out_specs=(VMEM,) * (1 + blanks),
        scratch_shapes=[
            pltpu.VMEM((3, 3, PACKED, LANES), F32),
            square,
            pltpu.VMEM((3, 2, 64, LANES), F32),
            pltpu.VMEM((S, S), F32),
            pltpu.VMEM((1, S), F32),
            region, region, tally, tally, region, tally,
            beside, beside, tally_beside, tally_beside,
            square,
            pltpu.VMEM((3, 3, ROWS, LANES), F32),
            pltpu.VMEM((2, S, BLK // 2 * LANES), F32),
            pltpu.VMEM((2 * S, 4 * S), BF16),
            pltpu.VMEM((2 * S, 2 * S), BF16),
            square,
            square,
            pltpu.VMEM((BLK, S, LANES), F32),
            pltpu.VMEM((2 * BLK, S, LANES), F32),
            pair, pair, single, single, single, single, pair, pair,
            pltpu.SemaphoreType.DMA((2, 4)),
            pltpu.SemaphoreType.DMA((6,)),
            pltpu.SemaphoreType.DMA((6,)),
            pltpu.SemaphoreType.DMA((2,)),
        ],
        compiler_params=pltpu.CompilerParams(collective_id=2 + step, has_side_effects=True, vmem_limit_bytes=LIMIT),
        name="exchange",
    )(moved, rates, mix, low, row, order, source, *sums)


def shards(species, reaction_rates, mix_rate, shift_list, arrival, cell_index):
    inputs = (pltpu.with_memory_space_constraint(x, pltpu.HBM) for x in (shift_list, arrival, species, cell_index))
    moved, row, low, place, source, *accs = migrate(*inputs)
    mix = mix_rate.reshape(1, S)
    for step in range(STEPS):
        sums, order = deposit(step, moved, low, row, place, accs)
        moved, *accs = exchange(step, sums, moved, reaction_rates, mix, low, row, order, source)
    return moved


def solution(mesh):
    placed = (
        P(("lat", "lon"), None, None),
        P(),
        P(),
        P(None, "lat", None),
        P(None, ("lat", "lon")),
        P(None, ("lat", "lon"), None),
    )
    return jax.shard_map(
        shards, mesh=mesh, in_specs=placed, out_specs=P(("lat", "lon"), None, None), check_vma=False
    )
```

```python
import functools

import jax
import jax.numpy as jnp
from jax import lax
from jax.experimental import pallas as pl
from jax.experimental.pallas import tpu as pltpu
from jax.sharding import PartitionSpec as P

S = 48
LANES = 128
BLK = 32
HALF_BLK = BLK // 2
CELL_DEV = 1024
ROWS = CELL_DEV // 2
STEPS = 2
SUB = 32
ACCS = 6
QUARTER = ROWS // 4
PACKED = 3 * QUARTER
PIECES = 6
PIECE = PACKED // PIECES
F32 = jnp.float32
BF16 = jnp.bfloat16
MESH = pl.DeviceIdType.MESH
VMEM = pl.BlockSpec(memory_space=pltpu.VMEM)
SMEM = pl.BlockSpec(memory_space=pltpu.SMEM)
HBM = pl.BlockSpec(memory_space=pltpu.HBM)
TABLE = jax.ShapeDtypeStruct((9 * ROWS, LANES), F32)
LIMIT = 24 * 2**20
BATCHES = (2, -2, 1, 1, -1, -1)
FIRST = {2: 0, -2: 1, 1: 2, -1: 4}
PLAN = (
    ("a", 0), ("a", 1), 1, ("a", 2), ("a", 3), 1, ("a", 4), ("a", 5), 1,
    ("o", 0), ("b", 0), ("o", 1), ("b", 1), 1, ("o", 2), ("b", 2), ("o", 3), ("b", 3), 1, ("o", 4), ("b", 4), ("o", 5), ("b", 5),
    1, ("c", 0), 1, ("c", 1), 1, ("c", 2), 1, ("c", 3), 1, ("c", 4), 1, ("c", 5), 2,
)
EARLY = 3


def around(axis, step):
    count = lax.axis_size(axis)
    return lax.rem(lax.axis_index(axis) + step + count, count)


def is_polar():
    band = lax.axis_index("lat")
    return (band == 0) | (band == lax.axis_size("lat") - 1)


def place_slots(shift_ref, step, unit, visit):
    def place(slot, counts):
        moved_by = shift_ref[step, 0, slot]
        where = 6 * unit + counts[4]
        later = []
        for offset, count in zip((2, -2, 1, -1), counts):
            hit = moved_by == offset
            where = jnp.where(hit, FIRST[offset] * unit + count, where)
            later.append(count + hit.astype(jnp.int32))
        later.append(counts[4] + (moved_by == 0).astype(jnp.int32))
        visit(slot, moved_by, jnp.minimum(where, BLK - 1))
        return tuple(later)

    lax.fori_loop(0, BLK, place, (jnp.int32(0),) * 5)


def batch_copy(pool, send_sem, recv_sem, k, unit):
    return pltpu.make_async_remote_copy(
        src_ref=pool.at[pl.ds(k * unit, unit)],
        dst_ref=pool.at[pl.ds(BLK + k * unit, unit)],
        send_sem=send_sem.at[k],
        recv_sem=recv_sem.at[k],
        device_id={"lon": around("lon", BATCHES[k])},
        device_id_type=MESH,
    )


def each_unit(polar, body):
    @pl.when(polar)
    def _():
        body(4)

    @pl.when(jnp.logical_not(polar))
    def _():
        body(2)


def blank_strips(refs):
    blank = jnp.zeros((8, LANES), F32)

    @pl.loop(0, 9 * ROWS // 8, unroll=4)
    def _(i):
        part = pl.ds(pl.multiple_of(i * 8, 8), 8)
        for ref in refs:
            ref[part, :] = blank


def migrate_kernel(shift_hbm, arrival_hbm, state_hbm, cell_hbm, moved_ref, row_ref, low_ref, place_ref, source_ref, *rest):
    accs = rest[:ACCS]
    shift_ref, arrival_ref, state_ref, cell_ref, pool, pool_at, load_sem, send_sem, recv_sem = rest[ACCS:]
    loads = [
        pltpu.make_async_copy(src, dst, load_sem.at[k])
        for k, (src, dst) in enumerate(
            ((shift_hbm, shift_ref), (arrival_hbm, arrival_ref), (state_hbm, state_ref), (cell_hbm, cell_ref))
        )
    ]
    for load in loads:
        load.start()
    polar = is_polar()
    unit = jnp.where(polar, 4, 2)
    barrier = pltpu.get_barrier_semaphore()
    for offset in (1, -1, 2, -2):
        pl.semaphore_signal(barrier, inc=1, device_id={"lon": around("lon", offset)}, device_id_type=MESH)

    def note(slot, moved_by, where):
        pool_at[slot] = where + jnp.where(moved_by == 0, 0, BLK)

    def note_later(slot, moved_by, where):
        place_ref[slot] = where + jnp.where(moved_by == 0, 0, BLK)

    loads[0].wait()
    place_slots(shift_ref, 0, unit, note)
    loads[1].wait()
    loads[2].wait()

    @pl.loop(0, 6 * unit)
    def _(where):
        def seek(slot, found):
            return jnp.where(pool_at[slot] == where + BLK, slot, found)

        pool[where] = state_ref[lax.fori_loop(0, BLK, seek, jnp.int32(0), unroll=True)]

    pl.semaphore_wait(barrier, 4)

    def start(unit):
        for k in range(6):
            batch_copy(pool, send_sem, recv_sem, k, unit).start()

    each_unit(polar, start)
    loads[3].wait()
    sectors = lax.axis_size("lon")
    cell = cell_ref[...]
    owner = cell // CELL_DEV
    rel_band = owner // sectors - lax.axis_index("lat") + 1
    rel_sector = (owner % sectors - lax.axis_index("lon") + 1 + sectors) % sectors
    row_ref[...] = jnp.clip((rel_band * 3 + rel_sector) * ROWS + cell % ROWS, 0, 9 * ROWS - 1)
    low_ref[...] = 1 - cell // ROWS % 2
    place_slots(shift_ref, STEPS - 1, unit, note_later)

    @pl.loop(0, BLK)
    def _(slot):
        source_ref[slot] = place_ref[arrival_ref[STEPS - 1, slot]]

    blank_strips(accs)

    def wait(unit):
        for k in range(6):
            batch_copy(pool, send_sem, recv_sem, k, unit).wait()

    each_unit(polar, wait)

    @pl.loop(0, BLK, unroll=4)
    def _(slot):
        old = arrival_ref[0, slot]
        at = pool_at[old]
        moved_ref[slot] = jnp.where(at < BLK, state_ref[old], pool[at])


def migrate(shift_list, arrival, state, cell_index):
    whole = jax.ShapeDtypeStruct((STEPS, BLK, LANES), jnp.int32)
    slots = jax.ShapeDtypeStruct((BLK,), jnp.int32)
    return pl.pallas_call(
        migrate_kernel,
        out_shape=(jax.ShapeDtypeStruct((BLK, S, LANES), F32), whole, whole, slots, slots) + (TABLE,) * ACCS,
        in_specs=[HBM] * 4,
        out_specs=(VMEM, VMEM, VMEM, SMEM, SMEM) + (VMEM,) * ACCS,
        scratch_shapes=[
            pltpu.SMEM((STEPS, 1, BLK), jnp.int32),
            pltpu.SMEM((STEPS, BLK), jnp.int32),
            pltpu.VMEM((BLK, S, LANES), F32),
            pltpu.VMEM((STEPS, BLK, LANES), jnp.int32),
            pltpu.VMEM((2 * BLK, S, LANES), F32),
            pltpu.SMEM((BLK,), jnp.int32),
            pltpu.SemaphoreType.DMA((4,)),
            pltpu.SemaphoreType.DMA((6,)),
            pltpu.SemaphoreType.DMA((6,)),
        ],
        compiler_params=pltpu.CompilerParams(collective_id=1, has_side_effects=True, vmem_limit_bytes=LIMIT),
        name="migrate",
    )(shift_list, arrival, state, cell_index)


def split(x):
    high = x.astype(BF16)
    return high, (x - high.astype(F32)).astype(BF16)


def pairs_of(rates):
    zero = jnp.zeros((S, S), F32)
    high, low = split(jnp.concatenate([jnp.concatenate([rates, zero], 1), jnp.concatenate([zero, rates], 1)], 0))
    return jnp.concatenate([high, high], 1), low


def substep(chem, high2, low1):
    state = chem[...].reshape(2 * S, HALF_BLK * LANES)
    high, low = split(state)
    pushed = jnp.dot(high2[...], jnp.concatenate([high, low], 0), preferred_element_type=F32)
    pushed = pushed + jnp.dot(low1[...], high, preferred_element_type=F32)
    chem[...] = (state + (2.0 / SUB) * jnp.tanh(pushed)).reshape(2, S, HALF_BLK * LANES)


def deposit_kernel(step, moved_ref, low_ref, row_ref, place_ref, rates_ref, *rest):
    accs = rest[ACCS:2 * ACCS]
    order_ref, chem, even, odd, high2, low1 = rest[2 * ACCS:]
    high2[...], low1[...] = pairs_of(rates_ref[...])
    for b in range(BLK):
        column = b % HALF_BLK * LANES
        chem[b // HALF_BLK, :, column:column + LANES] = moved_ref[b]
    tail = jnp.where(lax.broadcasted_iota(jnp.int32, (16, LANES), 0) == 0, 1.0, 0.0)

    def turn(b, rows):
        block = jnp.concatenate([moved_ref[b], tail], 0)
        low = low_ref[step, pl.ds(b, 1), :] == 1
        rows[...] = jnp.concatenate([jnp.where(low, block, 0.0), jnp.where(low, 0.0, block)], 0).T

    def add(b, rows):
        for k in range(LANES):
            acc = accs[k % ACCS]
            at = pl.ds(row_ref[step, b, k], 1)
            acc[at, :] = acc[at, :] + rows[k:k + 1, :]

    turn(0, even)

    @pl.loop(0, BLK // 2)
    def _(i):
        substep(chem, high2, low1)
        turn(2 * i + 1, odd)
        add(2 * i, even)
        turn(jnp.minimum(2 * i + 2, BLK - 1), even)
        add(2 * i + 1, odd)

    @pl.loop(0, BLK)
    def _(slot):
        order_ref[place_ref[slot] % BLK] = slot


def deposit(step, moved, low, row, place, rates, accs):
    *sums, order, chem = pl.pallas_call(
        functools.partial(deposit_kernel, step),
        out_shape=(TABLE,) * ACCS
        + (jax.ShapeDtypeStruct((BLK,), jnp.int32), jax.ShapeDtypeStruct((2, S, HALF_BLK * LANES), F32)),
        in_specs=[VMEM, VMEM, SMEM, SMEM, VMEM] + [VMEM] * ACCS,
        out_specs=(VMEM,) * ACCS + (SMEM, VMEM),
        input_output_aliases={5 + k: k for k in range(ACCS)},
        scratch_shapes=[
            pltpu.VMEM((LANES, LANES), F32),
            pltpu.VMEM((LANES, LANES), F32),
            pltpu.VMEM((2 * S, 4 * S), BF16),
            pltpu.VMEM((2 * S, 2 * S), BF16),
        ],
        compiler_params=pltpu.CompilerParams(vmem_limit_bytes=LIMIT),
        name="deposit",
    )(moved, low, row, place, rates, *accs)
    return sums, order, chem


def exchange_kernel(
    step, moved_ref, chem_ref, rates_hbm, mix_hbm, low_ref, row_ref, order_ref, source_ref, *rest
):
    last = step == STEPS - 1
    accs = rest[:ACCS]
    out_ref = rest[ACCS]
    blanks = () if last else rest[ACCS + 1:2 * ACCS + 1]
    (
        sums_ref, counts, tallies, rates_ref, mix_ref, below, above, tally_below, tally_above, middle, tally_middle,
        left, right, tally_left, tally_right, factors, table, chem, high2, low1, even, odd, reacted, pool,
        up_sem, down_sem, west_sem, east_sem, mwest_sem, meast_sem, mup_sem, mdown_sem, tally_sem, send_sem, recv_sem, load_sem,
    ) = rest[ACCS + 1 + len(blanks):]
    loads = [
        pltpu.make_async_copy(rates_hbm, rates_ref, load_sem.at[0]),
        pltpu.make_async_copy(mix_hbm, mix_ref, load_sem.at[1]),
    ]
    lane = lax.broadcasted_iota(jnp.int32, (8, LANES), 1)
    spot = lane % 64
    spare = spot >= S
    for load in loads:
        load.start()

    def add_up(r):
        @pl.loop(0, QUARTER // 8, unroll=4)
        def _(i):
            at = pl.multiple_of(i * 8, 8)
            tally = jnp.zeros((8, LANES), F32)
            for s in range(3):
                quarters = []
                for q in range(4):
                    part = pl.ds((r * 3 + s) * ROWS + q * QUARTER + at, 8)
                    total = accs[0][part, :]
                    for acc in accs[1:]:
                        total = total + acc[part, :]
                    quarters.append(total)
                    tally = jnp.where(spot == s * 8 + q, pltpu.roll(total, (s * 8 + q - S) % LANES, 1), tally)
                for q in range(3):
                    sums_ref[r, s, pl.ds(q * QUARTER + at, 8), :] = jnp.where(
                        spare, pltpu.roll(quarters[3], S - 16 * q, 1), quarters[q]
                    )
            counts[pl.ds(at, 8), :] = tally

        tallies[r] = counts[...].T.reshape(2, 64, LANES)

    band = lax.axis_index("lat")
    bands = lax.axis_size("lat")
    has_up = band < bands - 1
    has_down = band > 0
    up = jnp.minimum(band + 1, bands - 1)
    down = jnp.maximum(band - 1, 0)
    east = around("lon", 1)
    west = around("lon", -1)
    beside = (1, -1) if last else (1, -1, 2, -2)
    barrier = pltpu.get_barrier_semaphore()
    for offset in beside:
        pl.semaphore_signal(barrier, inc=1, device_id={"lon": around("lon", offset)}, device_id_type=MESH)

    @pl.when(has_up)
    def _():
        pl.semaphore_signal(barrier, inc=1, device_id={"lat": up}, device_id_type=MESH)

    @pl.when(has_down)
    def _():
        pl.semaphore_signal(barrier, inc=1, device_id={"lat": down}, device_id_type=MESH)

    add_up(2)
    add_up(0)
    pl.semaphore_wait(barrier, len(beside) + has_up.astype(jnp.int32) + has_down.astype(jnp.int32))

    def remote(src, dst, sem, index, device):
        return pltpu.make_async_remote_copy(
            src_ref=src, dst_ref=dst, send_sem=sem.at[(0,) + index], recv_sem=sem.at[(1,) + index],
            device_id=device, device_id_type=MESH,
        )

    def piece(p):
        return pl.ds(p * PIECE, PIECE)

    def sums_up(s, p):
        return remote(sums_ref.at[2, s, piece(p)], below.at[s, piece(p)], up_sem, (s, p), {"lat": up})

    def sums_down(s, p):
        return remote(sums_ref.at[0, s, piece(p)], above.at[s, piece(p)], down_sem, (s, p), {"lat": down})

    def sums_west(p):
        return remote(middle.at[0, piece(p)], right.at[piece(p)], west_sem, (p,), {"lon": west})

    def sums_east(p):
        return remote(middle.at[2, piece(p)], left.at[piece(p)], east_sem, (p,), {"lon": east})

    def means_west(p):
        return remote(table.at[1, 1, piece(p)], table.at[1, 2, piece(p)], mwest_sem, (p,), {"lon": west})

    def means_east(p):
        return remote(table.at[1, 1, piece(p)], table.at[1, 0, piece(p)], meast_sem, (p,), {"lon": east})

    def means_up(s, p):
        return remote(table.at[1, s, piece(p)], table.at[0, s, piece(p)], mup_sem, (s, p), {"lat": up})

    def means_down(s, p):
        return remote(table.at[1, s, piece(p)], table.at[2, s, piece(p)], mdown_sem, (s, p), {"lat": down})

    def tally_up():
        return remote(tallies.at[2, :, pl.ds(0, 24)], tally_below, tally_sem, (0,), {"lat": up})

    def tally_down():
        return remote(tallies.at[0, :, pl.ds(0, 24)], tally_above, tally_sem, (1,), {"lat": down})

    def tally_west():
        return remote(tally_middle.at[:, pl.ds(0, 8)], tally_right, tally_sem, (2,), {"lon": west})

    def tally_east():
        return remote(tally_middle.at[:, pl.ds(16, 8)], tally_left, tally_sem, (3,), {"lon": east})

    order = [(s, p) for p in range(PIECES) for s in (0, 2)] + [(1, p) for p in range(PIECES)]

    @pl.when(has_up)
    def _():
        tally_up().start()
        for s, p in order:
            sums_up(s, p).start()

    @pl.when(has_down)
    def _():
        tally_down().start()
        for s, p in order:
            sums_down(s, p).start()

    @pl.when(jnp.logical_not(has_down))
    def _():
        below[...] = jnp.zeros_like(below)
        tally_below[...] = jnp.zeros_like(tally_below)
        table[0] = jnp.zeros_like(table[0])

    @pl.when(jnp.logical_not(has_up))
    def _():
        above[...] = jnp.zeros_like(above)
        tally_above[...] = jnp.zeros_like(tally_above)
        table[2] = jnp.zeros_like(table[2])

    add_up(1)
    for load in loads:
        load.wait()
    high2[...], low1[...] = pairs_of(rates_ref[...])
    chem[...] = chem_ref[...]

    def chemistry(substeps):
        @pl.loop(0, substeps)
        def _(_):
            substep(chem, high2, low1)

    chemistry(EARLY)

    def strips(first, rows, body):
        @pl.loop(0, rows // 8, unroll=4)
        def _(i):
            body(pl.multiple_of(i * 8, 8) + first)

    def bands_summed(s, p):
        @pl.when(has_down)
        def _():
            sums_up(s, p).wait_recv()

        @pl.when(has_up)
        def _():
            sums_down(s, p).wait_recv()

        def add_bands(i):
            part = pl.ds(i, 8)
            middle[s, part, :] = sums_ref[1, s, part, :] + below[s, part, :] + above[s, part, :]

        strips(p * PIECE, PIECE, add_bands)

    def sides_summed(p):
        if p == 0:
            @pl.when(has_down)
            def _():
                tally_up().wait_recv()

            @pl.when(has_up)
            def _():
                tally_down().wait_recv()

            tally_middle[...] = tallies[1, :, 0:24] + tally_below[...] + tally_above[...]
            tally_west().start()
            tally_east().start()
        bands_summed(0, p)
        sums_west(p).start()
        bands_summed(2, p)
        sums_east(p).start()

    def own_summed(p):
        bands_summed(1, p)

    def sectors_summed(p):
        if p == 0:
            tally_west().wait_recv()
            tally_east().wait_recv()
            tally = tally_middle[:, 8:16] + tally_left[...] + tally_right[...]
            inverse = (1.0 / jnp.maximum(tally, 1.0)).reshape(16, LANES)
            factors[...] = jnp.concatenate([inverse, jnp.zeros((LANES - 16, LANES), F32)], 0).T
        sums_west(p).wait_recv()
        sums_east(p).wait_recv()
        q = p * PIECE // QUARTER

        def mean(i):
            part = pl.ds(i, 8)
            factor = factors[pl.ds(i - q * QUARTER, 8), :]
            low = jnp.where(spare, factor[:, 3:4], factor[:, q:q + 1])
            high = jnp.where(spare, factor[:, 11:12], factor[:, 8 + q:9 + q])
            total = middle[1, part, :] + left[part, :] + right[part, :]
            table[1, 1, part, :] = total * jnp.where(lane < 64, low, high)

        strips(p * PIECE, PIECE, mean)
        means_west(p).start()
        means_east(p).start()

        @pl.when(has_up)
        def _():
            means_up(1, p).start()

        @pl.when(has_down)
        def _():
            means_down(1, p).start()

    def means_passed(p):
        means_west(p).wait_recv()
        means_east(p).wait_recv()

        @pl.when(has_up)
        def _():
            means_up(0, p).start()
            means_up(2, p).start()

        @pl.when(has_down)
        def _():
            means_down(0, p).start()
            means_down(2, p).start()

    parts = {"a": sides_summed, "o": own_summed, "b": sectors_summed, "c": means_passed}
    for entry in PLAN:
        if isinstance(entry, int):
            chemistry(entry)
        else:
            parts[entry[0]](entry[1])

    if not last:
        blank_strips(blanks)
    for b in range(BLK):
        column = b % HALF_BLK * LANES
        reacted[b] = chem[b // HALF_BLK, :, column:column + LANES]

    def means_landed(sectors):
        @pl.when(has_up)
        def _():
            for s, p in order:
                if s in sectors:
                    means_down(s, p).wait_recv()

        @pl.when(has_down)
        def _():
            for s, p in order:
                if s in sectors:
                    means_up(s, p).wait_recv()

    def unpack_regions(regions):
        def unpack(i):
            for r, s in regions:
                found = [pltpu.roll(table[r, s, pl.ds(q * QUARTER + i, 8), :], LANES - S + 16 * q, 1) for q in range(3)]
                table[r, s, pl.ds(PACKED + i, 8), :] = jnp.where(spot < 16, found[0], jnp.where(spot < 32, found[1], found[2]))

        strips(0, QUARTER, unpack)

    unpack_regions([(1, 0), (1, 1), (1, 2)])
    means_landed((1,))
    unpack_regions([(0, 1), (2, 1)])
    means_landed((0, 2))
    unpack_regions([(0, 0), (0, 2), (2, 0), (2, 2)])

    mix = jnp.broadcast_to(mix_ref[...], (LANES, S)).T
    flat = table.reshape(9 * ROWS, LANES)

    def gather(b, rows):
        for k in range(LANES):
            rows[k:k + 1, :] = flat[pl.ds(row_ref[step, b, k], 1), :]

    def mixed(b, rows):
        means = rows[...].T
        low = low_ref[step, pl.ds(b, 1), :] == 1
        picked = jnp.where(low, means[0:S], means[64:64 + S])
        return reacted[b] + mix * (picked - moved_ref[b])

    def pair(order_of, target, i):
        first, second = order_of(2 * i), order_of(2 * i + 1)
        gather(first, even)
        gather(second, odd)
        target[2 * i] = mixed(first, even)
        target[2 * i + 1] = mixed(second, odd)

    @pl.when(has_up)
    def _():
        tally_up().wait_send()
        for s, p in order:
            sums_up(s, p).wait_send()
            means_up(s, p).wait_send()

    @pl.when(has_down)
    def _():
        tally_down().wait_send()
        for s, p in order:
            sums_down(s, p).wait_send()
            means_down(s, p).wait_send()

    tally_west().wait_send()
    tally_east().wait_send()
    for p in range(PIECES):
        for copy in (sums_west(p), sums_east(p), means_west(p), means_east(p)):
            copy.wait_send()

    if last:
        @pl.loop(0, BLK // 2)
        def _(i):
            pair(lambda b: b, out_ref, i)
    else:
        polar = is_polar()
        half_unit = jnp.where(polar, 2, 1)

        @pl.loop(0, 6)
        def _(k):
            @pl.loop(0, half_unit)
            def _(u):
                pair(lambda at: order_ref[at], pool, k * half_unit + u)

            for batch in range(6):
                @pl.when(k == batch)
                def _():
                    each_unit(polar, lambda unit: batch_copy(pool, send_sem, recv_sem, batch, unit).start())

        @pl.loop(6 * half_unit, BLK // 2)
        def _(i):
            pair(lambda at: order_ref[at], pool, i)

        def wait(unit):
            for k in range(6):
                batch_copy(pool, send_sem, recv_sem, k, unit).wait()

        each_unit(polar, wait)

        @pl.loop(0, BLK, unroll=4)
        def _(slot):
            out_ref[slot] = pool[source_ref[slot]]


def exchange(step, sums, moved, chem, rates, mix, low, row, order, source):
    region = pltpu.VMEM((3, PACKED, LANES), F32)
    beside = pltpu.VMEM((PACKED, LANES), F32)
    tally = pltpu.VMEM((2, 24, LANES), F32)
    tally_beside = pltpu.VMEM((2, 8, LANES), F32)
    square = pltpu.VMEM((LANES, LANES), F32)
    pair = pltpu.SemaphoreType.DMA((2, 3, PIECES))
    single = pltpu.SemaphoreType.DMA((2, PIECES))
    blanks = 0 if step == STEPS - 1 else ACCS
    state = jax.ShapeDtypeStruct((BLK, S, LANES), F32)
    return pl.pallas_call(
        functools.partial(exchange_kernel, step),
        out_shape=(state,) + (TABLE,) * blanks,
        in_specs=[VMEM, VMEM, HBM, HBM, VMEM, SMEM, SMEM, SMEM] + [VMEM] * ACCS,
        out_specs=(VMEM,) * (1 + blanks),
        scratch_shapes=[
            pltpu.VMEM((3, 3, PACKED, LANES), F32),
            square,
            pltpu.VMEM((3, 2, 64, LANES), F32),
            pltpu.VMEM((S, S), F32),
            pltpu.VMEM((1, S), F32),
            region, region, tally, tally, region, tally,
            beside, beside, tally_beside, tally_beside,
            square,
            pltpu.VMEM((3, 3, ROWS, LANES), F32),
            pltpu.VMEM((2, S, BLK // 2 * LANES), F32),
            pltpu.VMEM((2 * S, 4 * S), BF16),
            pltpu.VMEM((2 * S, 2 * S), BF16),
            square,
            square,
            pltpu.VMEM((BLK, S, LANES), F32),
            pltpu.VMEM((2 * BLK, S, LANES), F32),
            pair, pair, single, single, single, single, pair, pair,
            pltpu.SemaphoreType.DMA((2, 4)),
            pltpu.SemaphoreType.DMA((6,)),
            pltpu.SemaphoreType.DMA((6,)),
            pltpu.SemaphoreType.DMA((2,)),
        ],
        compiler_params=pltpu.CompilerParams(collective_id=2 + step, has_side_effects=True, vmem_limit_bytes=LIMIT),
        name="exchange",
    )(moved, chem, rates, mix, low, row, order, source, *sums)


def shards(species, reaction_rates, mix_rate, shift_list, arrival, cell_index):
    inputs = (pltpu.with_memory_space_constraint(x, pltpu.HBM) for x in (shift_list, arrival, species, cell_index))
    moved, row, low, place, source, *accs = migrate(*inputs)
    mix = mix_rate.reshape(1, S)
    for step in range(STEPS):
        sums, order, chem = deposit(step, moved, low, row, place, reaction_rates, accs)
        moved, *accs = exchange(step, sums, moved, chem, reaction_rates, mix, low, row, order, source)
    return moved


def solution(mesh):
    placed = (
        P(("lat", "lon"), None, None),
        P(),
        P(),
        P(None, "lat", None),
        P(None, ("lat", "lon")),
        P(None, ("lat", "lon"), None),
    )
    return jax.shard_map(
        shards, mesh=mesh, in_specs=placed, out_specs=P(("lat", "lon"), None, None), check_vma=False
    )
```

```python
import functools

import jax
import jax.numpy as jnp
from jax import lax
from jax.experimental import pallas as pl
from jax.experimental.pallas import tpu as pltpu
from jax.sharding import PartitionSpec as P

S = 48
LANES = 128
BLK = 32
HALF_BLK = BLK // 2
CELL_DEV = 1024
ROWS = CELL_DEV // 2
STEPS = 2
SUB = 32
ACCS = 6
QUARTER = ROWS // 4
PACKED = 3 * QUARTER
PIECES = 6
PIECE = PACKED // PIECES
F32 = jnp.float32
BF16 = jnp.bfloat16
MESH = pl.DeviceIdType.MESH
VMEM = pl.BlockSpec(memory_space=pltpu.VMEM)
SMEM = pl.BlockSpec(memory_space=pltpu.SMEM)
HBM = pl.BlockSpec(memory_space=pltpu.HBM)
TABLE = jax.ShapeDtypeStruct((9 * ROWS, LANES), F32)
LIMIT = 24 * 2**20
BATCHES = (2, -2, 1, 1, -1, -1)
FIRST = {2: 0, -2: 1, 1: 2, -1: 4}
PLAN = (
    ("a", 0), 1, ("a", 1), 1, ("a", 2), 1, ("a", 3), 1, ("a", 4), 1, ("a", 5), 1,
    ("o", 0), ("b", 0), ("o", 1), ("b", 1), 1, ("o", 2), ("b", 2), ("o", 3), ("b", 3), 1, ("o", 4), ("b", 4), ("o", 5), ("b", 5),
    3, ("c", 0), 1, ("c", 1), 1, ("c", 2), 1, ("c", 3), 1, ("c", 4), 1, ("c", 5), 4,
)
EARLY = 4


def around(axis, step):
    count = lax.axis_size(axis)
    return lax.rem(lax.axis_index(axis) + step + count, count)


def is_polar():
    band = lax.axis_index("lat")
    return (band == 0) | (band == lax.axis_size("lat") - 1)


def place_slots(shift_ref, step, unit, visit):
    def place(slot, counts):
        moved_by = shift_ref[step, 0, slot]
        where = 6 * unit + counts[4]
        later = []
        for offset, count in zip((2, -2, 1, -1), counts):
            hit = moved_by == offset
            where = jnp.where(hit, FIRST[offset] * unit + count, where)
            later.append(count + hit.astype(jnp.int32))
        later.append(counts[4] + (moved_by == 0).astype(jnp.int32))
        visit(slot, moved_by, jnp.minimum(where, BLK - 1))
        return tuple(later)

    lax.fori_loop(0, BLK, place, (jnp.int32(0),) * 5)


def batch_copy(pool, send_sem, recv_sem, k, unit):
    return pltpu.make_async_remote_copy(
        src_ref=pool.at[pl.ds(k * unit, unit)],
        dst_ref=pool.at[pl.ds(BLK + k * unit, unit)],
        send_sem=send_sem.at[k],
        recv_sem=recv_sem.at[k],
        device_id={"lon": around("lon", BATCHES[k])},
        device_id_type=MESH,
    )


def each_unit(polar, body):
    @pl.when(polar)
    def _():
        body(4)

    @pl.when(jnp.logical_not(polar))
    def _():
        body(2)


def blank_strips(refs):
    blank = jnp.zeros((8, LANES), F32)

    @pl.loop(0, 9 * ROWS // 8, unroll=4)
    def _(i):
        part = pl.ds(pl.multiple_of(i * 8, 8), 8)
        for ref in refs:
            ref[part, :] = blank


def migrate_kernel(
    shift_hbm, arrival_hbm, state_hbm, cell_hbm, rates_hbm, mix_hbm,
    moved_ref, row_ref, low_ref, place_ref, source_ref, rates_ref, mix_ref, *rest
):
    accs = rest[:ACCS]
    shift_ref, arrival_ref, state_ref, cell_ref, pool, pool_at, load_sem, send_sem, recv_sem = rest[ACCS:]
    loads = [
        pltpu.make_async_copy(src, dst, load_sem.at[k])
        for k, (src, dst) in enumerate(
            (
                (shift_hbm, shift_ref), (arrival_hbm, arrival_ref), (state_hbm, state_ref), (cell_hbm, cell_ref),
                (rates_hbm, rates_ref), (mix_hbm, mix_ref),
            )
        )
    ]
    for load in loads:
        load.start()
    polar = is_polar()
    unit = jnp.where(polar, 4, 2)
    barrier = pltpu.get_barrier_semaphore()
    for offset in (1, -1, 2, -2):
        pl.semaphore_signal(barrier, inc=1, device_id={"lon": around("lon", offset)}, device_id_type=MESH)

    def note(slot, moved_by, where):
        pool_at[slot] = where + jnp.where(moved_by == 0, 0, BLK)

    def note_later(slot, moved_by, where):
        place_ref[slot] = where + jnp.where(moved_by == 0, 0, BLK)

    loads[0].wait()
    place_slots(shift_ref, 0, unit, note)
    loads[1].wait()
    loads[2].wait()

    @pl.loop(0, 6 * unit)
    def _(where):
        def seek(slot, found):
            return jnp.where(pool_at[slot] == where + BLK, slot, found)

        pool[where] = state_ref[lax.fori_loop(0, BLK, seek, jnp.int32(0), unroll=True)]

    pl.semaphore_wait(barrier, 4)

    def start(unit):
        for k in range(6):
            batch_copy(pool, send_sem, recv_sem, k, unit).start()

    each_unit(polar, start)
    for load in loads[3:]:
        load.wait()
    sectors = lax.axis_size("lon")
    cell = cell_ref[...]
    owner = cell // CELL_DEV
    rel_band = owner // sectors - lax.axis_index("lat") + 1
    rel_sector = (owner % sectors - lax.axis_index("lon") + 1 + sectors) % sectors
    row_ref[...] = jnp.clip((rel_band * 3 + rel_sector) * ROWS + cell % ROWS, 0, 9 * ROWS - 1)
    low_ref[...] = 1 - cell // ROWS % 2
    place_slots(shift_ref, STEPS - 1, unit, note_later)

    @pl.loop(0, BLK)
    def _(slot):
        source_ref[slot] = place_ref[arrival_ref[STEPS - 1, slot]]

    blank_strips(accs)

    def wait(unit):
        for k in range(6):
            batch_copy(pool, send_sem, recv_sem, k, unit).wait()

    each_unit(polar, wait)

    @pl.loop(0, BLK, unroll=4)
    def _(slot):
        old = arrival_ref[0, slot]
        at = pool_at[old]
        moved_ref[slot] = jnp.where(at < BLK, state_ref[old], pool[at])


def migrate(shift_list, arrival, state, cell_index, rates, mix):
    whole = jax.ShapeDtypeStruct((STEPS, BLK, LANES), jnp.int32)
    slots = jax.ShapeDtypeStruct((BLK,), jnp.int32)
    return pl.pallas_call(
        migrate_kernel,
        out_shape=(jax.ShapeDtypeStruct((BLK, S, LANES), F32), whole, whole, slots, slots)
        + (jax.ShapeDtypeStruct((S, S), F32), jax.ShapeDtypeStruct((1, S), F32))
        + (TABLE,) * ACCS,
        in_specs=[HBM] * 6,
        out_specs=(VMEM, VMEM, VMEM, SMEM, SMEM, VMEM, VMEM) + (VMEM,) * ACCS,
        scratch_shapes=[
            pltpu.SMEM((STEPS, 1, BLK), jnp.int32),
            pltpu.SMEM((STEPS, BLK), jnp.int32),
            pltpu.VMEM((BLK, S, LANES), F32),
            pltpu.VMEM((STEPS, BLK, LANES), jnp.int32),
            pltpu.VMEM((2 * BLK, S, LANES), F32),
            pltpu.SMEM((BLK,), jnp.int32),
            pltpu.SemaphoreType.DMA((6,)),
            pltpu.SemaphoreType.DMA((6,)),
            pltpu.SemaphoreType.DMA((6,)),
        ],
        compiler_params=pltpu.CompilerParams(collective_id=1, has_side_effects=True, vmem_limit_bytes=LIMIT),
        name="migrate",
    )(shift_list, arrival, state, cell_index, rates, mix)


def split(x):
    high = x.astype(BF16)
    return high, (x - high.astype(F32)).astype(BF16)


def pairs_of(rates):
    zero = jnp.zeros((S, S), F32)
    high, low = split(jnp.concatenate([jnp.concatenate([rates, zero], 1), jnp.concatenate([zero, rates], 1)], 0))
    return jnp.concatenate([high, high], 1), low


def substep(chem, high2, low1):
    state = chem[...].reshape(2 * S, HALF_BLK * LANES)
    high, low = split(state)
    pushed = jnp.dot(high2[...], jnp.concatenate([high, low], 0), preferred_element_type=F32)
    pushed = pushed + jnp.dot(low1[...], high, preferred_element_type=F32)
    chem[...] = (state + (2.0 / SUB) * jnp.tanh(pushed)).reshape(2, S, HALF_BLK * LANES)


def deposit_kernel(step, moved_ref, low_ref, row_ref, place_ref, rates_ref, *rest):
    accs = rest[ACCS:2 * ACCS]
    order_ref, chem, even, odd, high2, low1 = rest[2 * ACCS:]
    high2[...], low1[...] = pairs_of(rates_ref[...])
    for b in range(BLK):
        column = b % HALF_BLK * LANES
        chem[b // HALF_BLK, :, column:column + LANES] = moved_ref[b]
    tail = jnp.where(lax.broadcasted_iota(jnp.int32, (16, LANES), 0) == 0, 1.0, 0.0)

    def turn(b, rows):
        block = jnp.concatenate([moved_ref[b], tail], 0)
        low = low_ref[step, pl.ds(b, 1), :] == 1
        rows[...] = jnp.concatenate([jnp.where(low, block, 0.0), jnp.where(low, 0.0, block)], 0).T

    def add(b, rows):
        for k in range(LANES):
            acc = accs[k % ACCS]
            at = pl.ds(row_ref[step, b, k], 1)
            acc[at, :] = acc[at, :] + rows[k:k + 1, :]

    turn(0, even)

    @pl.loop(0, BLK // 4)
    def _(i):
        substep(chem, high2, low1)
        turn(4 * i + 1, odd)
        add(4 * i, even)
        turn(4 * i + 2, even)
        add(4 * i + 1, odd)
        turn(4 * i + 3, odd)
        add(4 * i + 2, even)
        turn(jnp.minimum(4 * i + 4, BLK - 1), even)
        add(4 * i + 3, odd)

    @pl.loop(0, BLK)
    def _(slot):
        order_ref[place_ref[slot] % BLK] = slot


def deposit(step, moved, low, row, place, rates, accs):
    *sums, order, chem = pl.pallas_call(
        functools.partial(deposit_kernel, step),
        out_shape=(TABLE,) * ACCS
        + (jax.ShapeDtypeStruct((BLK,), jnp.int32), jax.ShapeDtypeStruct((2, S, HALF_BLK * LANES), F32)),
        in_specs=[VMEM, VMEM, SMEM, SMEM, VMEM] + [VMEM] * ACCS,
        out_specs=(VMEM,) * ACCS + (SMEM, VMEM),
        input_output_aliases={5 + k: k for k in range(ACCS)},
        scratch_shapes=[
            pltpu.VMEM((LANES, LANES), F32),
            pltpu.VMEM((LANES, LANES), F32),
            pltpu.VMEM((2 * S, 4 * S), BF16),
            pltpu.VMEM((2 * S, 2 * S), BF16),
        ],
        compiler_params=pltpu.CompilerParams(vmem_limit_bytes=LIMIT),
        name="deposit",
    )(moved, low, row, place, rates, *accs)
    return sums, order, chem


def exchange_kernel(
    step, moved_ref, chem_ref, rates_ref, mix_ref, low_ref, row_ref, order_ref, source_ref, *rest
):
    last = step == STEPS - 1
    accs = rest[:ACCS]
    out_ref = rest[ACCS]
    blanks = () if last else rest[ACCS + 1:2 * ACCS + 1]
    (
        sums_ref, counts, tallies, below, above, tally_below, tally_above, middle, tally_middle,
        left, right, tally_left, tally_right, factors, table, chem, high2, low1, even, odd, third, fourth, reacted, pool,
        up_sem, down_sem, west_sem, east_sem, mwest_sem, meast_sem, mup_sem, mdown_sem, tally_sem, send_sem, recv_sem,
    ) = rest[ACCS + 1 + len(blanks):]
    lane = lax.broadcasted_iota(jnp.int32, (8, LANES), 1)
    spot = lane % 64
    spare = spot >= S
    def add_up(r):
        @pl.loop(0, QUARTER // 8, unroll=4)
        def _(i):
            at = pl.multiple_of(i * 8, 8)
            tally = jnp.zeros((8, LANES), F32)
            for s in range(3):
                quarters = []
                for q in range(4):
                    part = pl.ds((r * 3 + s) * ROWS + q * QUARTER + at, 8)
                    total = accs[0][part, :]
                    for acc in accs[1:]:
                        total = total + acc[part, :]
                    quarters.append(total)
                    tally = jnp.where(spot == s * 8 + q, pltpu.roll(total, (s * 8 + q - S) % LANES, 1), tally)
                for q in range(3):
                    sums_ref[r, s, pl.ds(q * QUARTER + at, 8), :] = jnp.where(
                        spare, pltpu.roll(quarters[3], S - 16 * q, 1), quarters[q]
                    )
            counts[pl.ds(at, 8), :] = tally

        tallies[r] = counts[...].T.reshape(2, 64, LANES)

    band = lax.axis_index("lat")
    bands = lax.axis_size("lat")
    has_up = band < bands - 1
    has_down = band > 0
    up = jnp.minimum(band + 1, bands - 1)
    down = jnp.maximum(band - 1, 0)
    east = around("lon", 1)
    west = around("lon", -1)
    beside = (1, -1) if last else (1, -1, 2, -2)
    barrier = pltpu.get_barrier_semaphore()
    for offset in beside:
        pl.semaphore_signal(barrier, inc=1, device_id={"lon": around("lon", offset)}, device_id_type=MESH)

    @pl.when(has_up)
    def _():
        pl.semaphore_signal(barrier, inc=1, device_id={"lat": up}, device_id_type=MESH)

    @pl.when(has_down)
    def _():
        pl.semaphore_signal(barrier, inc=1, device_id={"lat": down}, device_id_type=MESH)

    add_up(2)
    add_up(0)
    pl.semaphore_wait(barrier, len(beside) + has_up.astype(jnp.int32) + has_down.astype(jnp.int32))

    def remote(src, dst, sem, index, device):
        return pltpu.make_async_remote_copy(
            src_ref=src, dst_ref=dst, send_sem=sem.at[(0,) + index], recv_sem=sem.at[(1,) + index],
            device_id=device, device_id_type=MESH,
        )

    def piece(p):
        return pl.ds(p * PIECE, PIECE)

    def sums_up(s, p):
        return remote(sums_ref.at[2, s, piece(p)], below.at[s, piece(p)], up_sem, (s, p), {"lat": up})

    def sums_down(s, p):
        return remote(sums_ref.at[0, s, piece(p)], above.at[s, piece(p)], down_sem, (s, p), {"lat": down})

    def sums_west(p):
        return remote(middle.at[0, piece(p)], right.at[piece(p)], west_sem, (p,), {"lon": west})

    def sums_east(p):
        return remote(middle.at[2, piece(p)], left.at[piece(p)], east_sem, (p,), {"lon": east})

    def means_west(p):
        return remote(table.at[1, 1, piece(p)], table.at[1, 2, piece(p)], mwest_sem, (p,), {"lon": west})

    def means_east(p):
        return remote(table.at[1, 1, piece(p)], table.at[1, 0, piece(p)], meast_sem, (p,), {"lon": east})

    def means_up(s, p):
        return remote(table.at[1, s, piece(p)], table.at[0, s, piece(p)], mup_sem, (s, p), {"lat": up})

    def means_down(s, p):
        return remote(table.at[1, s, piece(p)], table.at[2, s, piece(p)], mdown_sem, (s, p), {"lat": down})

    def tally_up():
        return remote(tallies.at[2, :, pl.ds(0, 24)], tally_below, tally_sem, (0,), {"lat": up})

    def tally_down():
        return remote(tallies.at[0, :, pl.ds(0, 24)], tally_above, tally_sem, (1,), {"lat": down})

    def tally_west():
        return remote(tally_middle.at[:, pl.ds(0, 8)], tally_right, tally_sem, (2,), {"lon": west})

    def tally_east():
        return remote(tally_middle.at[:, pl.ds(16, 8)], tally_left, tally_sem, (3,), {"lon": east})

    order = [(s, p) for p in range(PIECES) for s in (0, 2)] + [(1, p) for p in range(PIECES)]

    @pl.when(has_up)
    def _():
        tally_up().start()
        for s, p in order:
            sums_up(s, p).start()

    @pl.when(has_down)
    def _():
        tally_down().start()
        for s, p in order:
            sums_down(s, p).start()

    @pl.when(jnp.logical_not(has_down))
    def _():
        below[...] = jnp.zeros_like(below)
        tally_below[...] = jnp.zeros_like(tally_below)
        table[0] = jnp.zeros_like(table[0])

    @pl.when(jnp.logical_not(has_up))
    def _():
        above[...] = jnp.zeros_like(above)
        tally_above[...] = jnp.zeros_like(tally_above)
        table[2] = jnp.zeros_like(table[2])

    add_up(1)
    high2[...], low1[...] = pairs_of(rates_ref[...])
    chem[...] = chem_ref[...]

    def chemistry(substeps):
        @pl.loop(0, substeps)
        def _(_):
            substep(chem, high2, low1)

    chemistry(EARLY)

    def strips(first, rows, body):
        @pl.loop(0, rows // 8, unroll=4)
        def _(i):
            body(pl.multiple_of(i * 8, 8) + first)

    def bands_summed(s, p):
        @pl.when(has_down)
        def _():
            sums_up(s, p).wait_recv()

        @pl.when(has_up)
        def _():
            sums_down(s, p).wait_recv()

        def add_bands(i):
            part = pl.ds(i, 8)
            middle[s, part, :] = sums_ref[1, s, part, :] + below[s, part, :] + above[s, part, :]

        strips(p * PIECE, PIECE, add_bands)

    def sides_summed(p):
        if p == 0:
            @pl.when(has_down)
            def _():
                tally_up().wait_recv()

            @pl.when(has_up)
            def _():
                tally_down().wait_recv()

            tally_middle[...] = tallies[1, :, 0:24] + tally_below[...] + tally_above[...]
            tally_west().start()
            tally_east().start()
        bands_summed(0, p)
        sums_west(p).start()
        bands_summed(2, p)
        sums_east(p).start()

    def own_summed(p):
        bands_summed(1, p)

    def sectors_summed(p):
        if p == 0:
            tally_west().wait_recv()
            tally_east().wait_recv()
            tally = tally_middle[:, 8:16] + tally_left[...] + tally_right[...]
            inverse = (1.0 / jnp.maximum(tally, 1.0)).reshape(16, LANES)
            factors[...] = jnp.concatenate([inverse, jnp.zeros((LANES - 16, LANES), F32)], 0).T
        sums_west(p).wait_recv()
        sums_east(p).wait_recv()
        q = p * PIECE // QUARTER

        def mean(i):
            part = pl.ds(i, 8)
            factor = factors[pl.ds(i - q * QUARTER, 8), :]
            low = jnp.where(spare, factor[:, 3:4], factor[:, q:q + 1])
            high = jnp.where(spare, factor[:, 11:12], factor[:, 8 + q:9 + q])
            total = middle[1, part, :] + left[part, :] + right[part, :]
            table[1, 1, part, :] = total * jnp.where(lane < 64, low, high)

        strips(p * PIECE, PIECE, mean)
        means_west(p).start()
        means_east(p).start()

        @pl.when(has_up)
        def _():
            means_up(1, p).start()

        @pl.when(has_down)
        def _():
            means_down(1, p).start()

    def means_passed(p):
        means_west(p).wait_recv()
        means_east(p).wait_recv()

        @pl.when(has_up)
        def _():
            means_up(0, p).start()
            means_up(2, p).start()

        @pl.when(has_down)
        def _():
            means_down(0, p).start()
            means_down(2, p).start()

    parts = {"a": sides_summed, "o": own_summed, "b": sectors_summed, "c": means_passed}
    for entry in PLAN:
        if isinstance(entry, int):
            chemistry(entry)
        else:
            parts[entry[0]](entry[1])

    if not last:
        blank_strips(blanks)
    for b in range(BLK):
        column = b % HALF_BLK * LANES
        reacted[b] = chem[b // HALF_BLK, :, column:column + LANES]

    def means_landed(sectors):
        @pl.when(has_up)
        def _():
            for s, p in order:
                if s in sectors:
                    means_down(s, p).wait_recv()

        @pl.when(has_down)
        def _():
            for s, p in order:
                if s in sectors:
                    means_up(s, p).wait_recv()

    def unpack_regions(regions):
        def unpack(i):
            for r, s in regions:
                found = [pltpu.roll(table[r, s, pl.ds(q * QUARTER + i, 8), :], LANES - S + 16 * q, 1) for q in range(3)]
                table[r, s, pl.ds(PACKED + i, 8), :] = jnp.where(spot < 16, found[0], jnp.where(spot < 32, found[1], found[2]))

        strips(0, QUARTER, unpack)

    unpack_regions([(1, 0), (1, 1), (1, 2)])
    means_landed((1,))
    unpack_regions([(0, 1), (2, 1)])
    means_landed((0, 2))
    unpack_regions([(0, 0), (0, 2), (2, 0), (2, 2)])

    mix = jnp.broadcast_to(mix_ref[...], (LANES, S)).T
    flat = table.reshape(9 * ROWS, LANES)

    def gather(b, rows):
        for k in range(LANES):
            rows[k:k + 1, :] = flat[pl.ds(row_ref[step, b, k], 1), :]

    def mixed(b, rows):
        means = rows[...].T
        low = low_ref[step, pl.ds(b, 1), :] == 1
        picked = jnp.where(low, means[0:S], means[64:64 + S])
        return reacted[b] + mix * (picked - moved_ref[b])

    def pair(order_of, target, i):
        first, second = order_of(2 * i), order_of(2 * i + 1)
        gather(first, even)
        gather(second, odd)
        target[2 * i] = mixed(first, even)
        target[2 * i + 1] = mixed(second, odd)

    @pl.when(has_up)
    def _():
        tally_up().wait_send()
        for s, p in order:
            sums_up(s, p).wait_send()
            means_up(s, p).wait_send()

    @pl.when(has_down)
    def _():
        tally_down().wait_send()
        for s, p in order:
            sums_down(s, p).wait_send()
            means_down(s, p).wait_send()

    tally_west().wait_send()
    tally_east().wait_send()
    for p in range(PIECES):
        for copy in (sums_west(p), sums_east(p), means_west(p), means_east(p)):
            copy.wait_send()

    if last:
        @pl.loop(0, BLK // 4)
        def _(i):
            for k, rows in enumerate((even, odd, third, fourth)):
                gather(4 * i + k, rows)
            for k, rows in enumerate((even, odd, third, fourth)):
                out_ref[4 * i + k] = mixed(4 * i + k, rows)
    else:
        polar = is_polar()
        half_unit = jnp.where(polar, 2, 1)

        @pl.loop(0, 6)
        def _(k):
            @pl.loop(0, half_unit)
            def _(u):
                pair(lambda at: order_ref[at], pool, k * half_unit + u)

            for batch in range(6):
                @pl.when(k == batch)
                def _():
                    each_unit(polar, lambda unit: batch_copy(pool, send_sem, recv_sem, batch, unit).start())

        @pl.loop(6 * half_unit, BLK // 2)
        def _(i):
            pair(lambda at: order_ref[at], pool, i)

        def wait(unit):
            for k in range(6):
                batch_copy(pool, send_sem, recv_sem, k, unit).wait()

        each_unit(polar, wait)

        @pl.loop(0, BLK, unroll=4)
        def _(slot):
            out_ref[slot] = pool[source_ref[slot]]


def exchange(step, sums, moved, chem, rates, mix, low, row, order, source):
    region = pltpu.VMEM((3, PACKED, LANES), F32)
    beside = pltpu.VMEM((PACKED, LANES), F32)
    tally = pltpu.VMEM((2, 24, LANES), F32)
    tally_beside = pltpu.VMEM((2, 8, LANES), F32)
    square = pltpu.VMEM((LANES, LANES), F32)
    pair = pltpu.SemaphoreType.DMA((2, 3, PIECES))
    single = pltpu.SemaphoreType.DMA((2, PIECES))
    blanks = 0 if step == STEPS - 1 else ACCS
    state = jax.ShapeDtypeStruct((BLK, S, LANES), F32)
    return pl.pallas_call(
        functools.partial(exchange_kernel, step),
        out_shape=(state,) + (TABLE,) * blanks,
        in_specs=[VMEM, VMEM, VMEM, VMEM, VMEM, SMEM, SMEM, SMEM] + [VMEM] * ACCS,
        out_specs=(VMEM,) * (1 + blanks),
        scratch_shapes=[
            pltpu.VMEM((3, 3, PACKED, LANES), F32),
            square,
            pltpu.VMEM((3, 2, 64, LANES), F32),
            region, region, tally, tally, region, tally,
            beside, beside, tally_beside, tally_beside,
            square,
            pltpu.VMEM((3, 3, ROWS, LANES), F32),
            pltpu.VMEM((2, S, BLK // 2 * LANES), F32),
            pltpu.VMEM((2 * S, 4 * S), BF16),
            pltpu.VMEM((2 * S, 2 * S), BF16),
            square, square, square, square,
            pltpu.VMEM((BLK, S, LANES), F32),
            pltpu.VMEM((2 * BLK, S, LANES), F32),
            pair, pair, single, single, single, single, pair, pair,
            pltpu.SemaphoreType.DMA((2, 4)),
            pltpu.SemaphoreType.DMA((6,)),
            pltpu.SemaphoreType.DMA((6,)),
        ],
        compiler_params=pltpu.CompilerParams(collective_id=2 + step, has_side_effects=True, vmem_limit_bytes=LIMIT),
        name="exchange",
    )(moved, chem, rates, mix, low, row, order, source, *sums)


def shards(species, reaction_rates, mix_rate, shift_list, arrival, cell_index):
    inputs = (shift_list, arrival, species, cell_index, reaction_rates, mix_rate.reshape(1, S))
    inputs = (pltpu.with_memory_space_constraint(x, pltpu.HBM) for x in inputs)
    moved, row, low, place, source, rates, mix, *accs = migrate(*inputs)
    for step in range(STEPS):
        sums, order, chem = deposit(step, moved, low, row, place, rates, accs)
        moved, *accs = exchange(step, sums, moved, chem, rates, mix, low, row, order, source)
    return moved


def solution(mesh):
    placed = (
        P(("lat", "lon"), None, None),
        P(),
        P(),
        P(None, "lat", None),
        P(None, ("lat", "lon")),
        P(None, ("lat", "lon"), None),
    )
    return jax.shard_map(
        shards, mesh=mesh, in_specs=placed, out_specs=P(("lat", "lon"), None, None), check_vma=False
    )
```

```python
import functools

import jax
import jax.numpy as jnp
from jax import lax
from jax.experimental import pallas as pl
from jax.experimental.pallas import tpu as pltpu
from jax.sharding import PartitionSpec as P

S = 48
LANES = 128
BLK = 32
HALF_BLK = BLK // 2
CELL_DEV = 1024
ROWS = CELL_DEV // 2
STEPS = 2
SUB = 32
ACCS = 5
QUARTER = ROWS // 4
PACKED = 3 * QUARTER
PIECES = 6
PIECE = PACKED // PIECES
F32 = jnp.float32
BF16 = jnp.bfloat16
MESH = pl.DeviceIdType.MESH
VMEM = pl.BlockSpec(memory_space=pltpu.VMEM)
SMEM = pl.BlockSpec(memory_space=pltpu.SMEM)
HBM = pl.BlockSpec(memory_space=pltpu.HBM)
TABLE = jax.ShapeDtypeStruct((9 * ROWS, LANES), F32)
LIMIT = 24 * 2**20
BATCHES = (2, -2, 1, 1, -1, -1)
FIRST = {2: 0, -2: 1, 1: 2, -1: 4}
PLAN = (('a', 0), 1, ('a', 1), 1, ('a', 2), 1, ('a', 3), 1, ('a', 4), 1, ('a', 5), 1, ('o', 0), ('b', 0), ('o', 1), ('b', 1), 1, ('o', 2), ('b', 2), ('o', 3), ('b', 3), 1, ('o', 4), ('b', 4), ('o', 5), ('b', 5), 4, ('c', 0), 1, ('c', 1), 1, ('c', 2), 1, ('c', 3), 1, ('c', 4), 1, ('c', 5), 2)
EARLY = 5


def around(axis, step):
    count = lax.axis_size(axis)
    return lax.rem(lax.axis_index(axis) + step + count, count)


def is_polar():
    band = lax.axis_index("lat")
    return (band == 0) | (band == lax.axis_size("lat") - 1)


def place_slots(shift_ref, step, unit, visit):
    def place(slot, counts):
        moved_by = shift_ref[step, 0, slot]
        where = 6 * unit + counts[4]
        later = []
        for offset, count in zip((2, -2, 1, -1), counts):
            hit = moved_by == offset
            where = jnp.where(hit, FIRST[offset] * unit + count, where)
            later.append(count + hit.astype(jnp.int32))
        later.append(counts[4] + (moved_by == 0).astype(jnp.int32))
        visit(slot, moved_by, jnp.minimum(where, BLK - 1))
        return tuple(later)

    lax.fori_loop(0, BLK, place, (jnp.int32(0),) * 5)


def batch_copy(pool, send_sem, recv_sem, k, unit):
    return pltpu.make_async_remote_copy(
        src_ref=pool.at[pl.ds(k * unit, unit)],
        dst_ref=pool.at[pl.ds(BLK + k * unit, unit)],
        send_sem=send_sem.at[k],
        recv_sem=recv_sem.at[k],
        device_id={"lon": around("lon", BATCHES[k])},
        device_id_type=MESH,
    )


def each_unit(polar, body):
    @pl.when(polar)
    def _():
        body(4)

    @pl.when(jnp.logical_not(polar))
    def _():
        body(2)


def blank_strips(refs):
    blank = jnp.zeros((8, LANES), F32)

    @pl.loop(0, 9 * ROWS // 8, unroll=4)
    def _(i):
        part = pl.ds(pl.multiple_of(i * 8, 8), 8)
        for ref in refs:
            ref[part, :] = blank


def migrate_kernel(
    shift_hbm, arrival_hbm, state_hbm, cell_hbm, rates_hbm, mix_hbm,
    moved_ref, row_ref, low_ref, place_ref, source_ref, rates_ref, mix_ref, *rest
):
    accs = rest[:ACCS]
    shift_ref, arrival_ref, state_ref, cell_ref, pool, pool_at, load_sem, send_sem, recv_sem = rest[ACCS:]
    loads = [
        pltpu.make_async_copy(src, dst, load_sem.at[k])
        for k, (src, dst) in enumerate(
            (
                (shift_hbm, shift_ref), (arrival_hbm, arrival_ref), (state_hbm, state_ref), (cell_hbm, cell_ref),
                (rates_hbm, rates_ref), (mix_hbm, mix_ref),
            )
        )
    ]
    for load in loads:
        load.start()
    polar = is_polar()
    unit = jnp.where(polar, 4, 2)
    barrier = pltpu.get_barrier_semaphore()
    for offset in (1, -1, 2, -2):
        pl.semaphore_signal(barrier, inc=1, device_id={"lon": around("lon", offset)}, device_id_type=MESH)

    def note(slot, moved_by, where):
        pool_at[slot] = where + jnp.where(moved_by == 0, 0, BLK)

    def note_later(slot, moved_by, where):
        place_ref[slot] = where + jnp.where(moved_by == 0, 0, BLK)

    loads[0].wait()
    place_slots(shift_ref, 0, unit, note)
    loads[1].wait()
    loads[2].wait()

    pl.semaphore_wait(barrier, 4)

    def start(unit):
        for k in range(6):
            @pl.loop(k * unit, k * unit + unit)
            def _(where):
                def seek(slot, found):
                    return jnp.where(pool_at[slot] == where + BLK, slot, found)

                pool[where] = state_ref[lax.fori_loop(0, BLK, seek, jnp.int32(0), unroll=True)]

            batch_copy(pool, send_sem, recv_sem, k, unit).start()

    each_unit(polar, start)
    for load in loads[3:]:
        load.wait()
    sectors = lax.axis_size("lon")
    cell = cell_ref[...]
    owner = cell // CELL_DEV
    rel_band = owner // sectors - lax.axis_index("lat") + 1
    rel_sector = (owner % sectors - lax.axis_index("lon") + 1 + sectors) % sectors
    row_ref[...] = jnp.clip((rel_band * 3 + rel_sector) * ROWS + cell % ROWS, 0, 9 * ROWS - 1)
    low_ref[...] = 1 - cell // ROWS % 2
    place_slots(shift_ref, STEPS - 1, unit, note_later)

    @pl.loop(0, BLK)
    def _(slot):
        source_ref[slot] = place_ref[arrival_ref[STEPS - 1, slot]]

    blank_strips(accs)

    def wait(unit):
        for k in range(6):
            batch_copy(pool, send_sem, recv_sem, k, unit).wait()

    each_unit(polar, wait)

    @pl.loop(0, BLK, unroll=4)
    def _(slot):
        old = arrival_ref[0, slot]
        at = pool_at[old]
        moved_ref[slot] = jnp.where(at < BLK, state_ref[old], pool[at])


def migrate(shift_list, arrival, state, cell_index, rates, mix):
    whole = jax.ShapeDtypeStruct((STEPS, BLK, LANES), jnp.int32)
    slots = jax.ShapeDtypeStruct((BLK,), jnp.int32)
    return pl.pallas_call(
        migrate_kernel,
        out_shape=(jax.ShapeDtypeStruct((BLK, S, LANES), F32), whole, whole, slots, slots)
        + (jax.ShapeDtypeStruct((S, S), F32), jax.ShapeDtypeStruct((1, S), F32))
        + (TABLE,) * ACCS,
        in_specs=[HBM] * 6,
        out_specs=(VMEM, VMEM, VMEM, SMEM, SMEM, VMEM, VMEM) + (VMEM,) * ACCS,
        scratch_shapes=[
            pltpu.SMEM((STEPS, 1, BLK), jnp.int32),
            pltpu.SMEM((STEPS, BLK), jnp.int32),
            pltpu.VMEM((BLK, S, LANES), F32),
            pltpu.VMEM((STEPS, BLK, LANES), jnp.int32),
            pltpu.VMEM((2 * BLK, S, LANES), F32),
            pltpu.SMEM((BLK,), jnp.int32),
            pltpu.SemaphoreType.DMA((6,)),
            pltpu.SemaphoreType.DMA((6,)),
            pltpu.SemaphoreType.DMA((6,)),
        ],
        compiler_params=pltpu.CompilerParams(collective_id=1, has_side_effects=True, vmem_limit_bytes=LIMIT),
        name="migrate",
    )(shift_list, arrival, state, cell_index, rates, mix)


def split(x):
    high = x.astype(BF16)
    return high, (x - high.astype(F32)).astype(BF16)


def pairs_of(rates):
    zero = jnp.zeros((S, S), F32)
    high, low = split(jnp.concatenate([jnp.concatenate([rates, zero], 1), jnp.concatenate([zero, rates], 1)], 0))
    return jnp.concatenate([high, high], 1), low


def substep(chem, high2, low1):
    state = chem[...].reshape(2 * S, HALF_BLK * LANES)
    high, low = split(state)
    pushed = jnp.dot(high2[...], jnp.concatenate([high, low], 0), preferred_element_type=F32)
    pushed = pushed + jnp.dot(low1[...], high, preferred_element_type=F32)
    chem[...] = (state + (2.0 / SUB) * jnp.tanh(pushed)).reshape(2, S, HALF_BLK * LANES)


def deposit_kernel(step, moved_ref, low_ref, row_ref, place_ref, rates_ref, *rest):
    accs = rest[ACCS:2 * ACCS]
    order_ref, chem, even, odd, high2, low1 = rest[2 * ACCS:]
    high2[...], low1[...] = pairs_of(rates_ref[...])
    for b in range(BLK):
        column = b % HALF_BLK * LANES
        chem[b // HALF_BLK, :, column:column + LANES] = moved_ref[b]
    tail = jnp.where(lax.broadcasted_iota(jnp.int32, (16, LANES), 0) == 0, 1.0, 0.0)

    def turn(b, rows):
        block = jnp.concatenate([moved_ref[b], tail], 0)
        low = low_ref[step, pl.ds(b, 1), :] == 1
        rows[...] = jnp.concatenate([jnp.where(low, block, 0.0), jnp.where(low, 0.0, block)], 0).T

    def add(b, rows):
        for k in range(LANES):
            acc = accs[k % ACCS]
            at = pl.ds(row_ref[step, b, k], 1)
            acc[at, :] = acc[at, :] + rows[k:k + 1, :]

    turn(0, even)

    @pl.loop(0, BLK // 4)
    def _(i):
        substep(chem, high2, low1)
        turn(4 * i + 1, odd)
        add(4 * i, even)
        turn(4 * i + 2, even)
        add(4 * i + 1, odd)
        turn(4 * i + 3, odd)
        add(4 * i + 2, even)
        turn(jnp.minimum(4 * i + 4, BLK - 1), even)
        add(4 * i + 3, odd)

    @pl.loop(0, BLK)
    def _(slot):
        order_ref[place_ref[slot] % BLK] = slot


def deposit(step, moved, low, row, place, rates, accs):
    *sums, order, chem = pl.pallas_call(
        functools.partial(deposit_kernel, step),
        out_shape=(TABLE,) * ACCS
        + (jax.ShapeDtypeStruct((BLK,), jnp.int32), jax.ShapeDtypeStruct((2, S, HALF_BLK * LANES), F32)),
        in_specs=[VMEM, VMEM, SMEM, SMEM, VMEM] + [VMEM] * ACCS,
        out_specs=(VMEM,) * ACCS + (SMEM, VMEM),
        input_output_aliases={5 + k: k for k in range(ACCS)},
        scratch_shapes=[
            pltpu.VMEM((LANES, LANES), F32),
            pltpu.VMEM((LANES, LANES), F32),
            pltpu.VMEM((2 * S, 4 * S), BF16),
            pltpu.VMEM((2 * S, 2 * S), BF16),
        ],
        compiler_params=pltpu.CompilerParams(vmem_limit_bytes=LIMIT),
        name="deposit",
    )(moved, low, row, place, rates, *accs)
    return sums, order, chem


def exchange_kernel(
    step, moved_ref, chem_ref, rates_ref, mix_ref, low_ref, row_ref, order_ref, source_ref, *rest
):
    last = step == STEPS - 1
    accs = rest[:ACCS]
    out_ref = rest[ACCS]
    blanks = () if last else rest[ACCS + 1:2 * ACCS + 1]
    (
        sums_ref, counts, tallies, below, above, tally_below, tally_above, middle, tally_middle,
        left, right, tally_left, tally_right, factors, table, chem, high2, low1, even, odd, third, fourth, reacted, pool,
        up_sem, down_sem, west_sem, east_sem, mwest_sem, meast_sem, mup_sem, mdown_sem, tally_sem, send_sem, recv_sem,
    ) = rest[ACCS + 1 + len(blanks):]
    lane = lax.broadcasted_iota(jnp.int32, (8, LANES), 1)
    spot = lane % 64
    spare = spot >= S
    def add_up(r):
        @pl.loop(0, QUARTER // 8, unroll=4)
        def _(i):
            at = pl.multiple_of(i * 8, 8)
            tally = jnp.zeros((8, LANES), F32)
            for s in range(3):
                quarters = []
                for q in range(4):
                    part = pl.ds((r * 3 + s) * ROWS + q * QUARTER + at, 8)
                    total = accs[0][part, :]
                    for acc in accs[1:]:
                        total = total + acc[part, :]
                    quarters.append(total)
                    tally = jnp.where(spot == s * 8 + q, pltpu.roll(total, (s * 8 + q - S) % LANES, 1), tally)
                for q in range(3):
                    sums_ref[r, s, pl.ds(q * QUARTER + at, 8), :] = jnp.where(
                        spare, pltpu.roll(quarters[3], S - 16 * q, 1), quarters[q]
                    )
            counts[pl.ds(at, 8), :] = tally

        tallies[r] = counts[...].T.reshape(2, 64, LANES)

    band = lax.axis_index("lat")
    bands = lax.axis_size("lat")
    has_up = band < bands - 1
    has_down = band > 0
    up = jnp.minimum(band + 1, bands - 1)
    down = jnp.maximum(band - 1, 0)
    east = around("lon", 1)
    west = around("lon", -1)
    beside = (1, -1) if last else (1, -1, 2, -2)
    barrier = pltpu.get_barrier_semaphore()
    for offset in beside:
        pl.semaphore_signal(barrier, inc=1, device_id={"lon": around("lon", offset)}, device_id_type=MESH)

    @pl.when(has_up)
    def _():
        pl.semaphore_signal(barrier, inc=1, device_id={"lat": up}, device_id_type=MESH)

    @pl.when(has_down)
    def _():
        pl.semaphore_signal(barrier, inc=1, device_id={"lat": down}, device_id_type=MESH)

    add_up(2)
    add_up(0)
    pl.semaphore_wait(barrier, len(beside) + has_up.astype(jnp.int32) + has_down.astype(jnp.int32))

    def remote(src, dst, sem, index, device):
        return pltpu.make_async_remote_copy(
            src_ref=src, dst_ref=dst, send_sem=sem.at[(0,) + index], recv_sem=sem.at[(1,) + index],
            device_id=device, device_id_type=MESH,
        )

    def piece(p):
        return pl.ds(p * PIECE, PIECE)

    def sums_up(s, p):
        return remote(sums_ref.at[2, s, piece(p)], below.at[s, piece(p)], up_sem, (s, p), {"lat": up})

    def sums_down(s, p):
        return remote(sums_ref.at[0, s, piece(p)], above.at[s, piece(p)], down_sem, (s, p), {"lat": down})

    def sums_west(p):
        return remote(middle.at[0, piece(p)], right.at[piece(p)], west_sem, (p,), {"lon": west})

    def sums_east(p):
        return remote(middle.at[2, piece(p)], left.at[piece(p)], east_sem, (p,), {"lon": east})

    def means_west(p):
        return remote(table.at[1, 1, piece(p)], table.at[1, 2, piece(p)], mwest_sem, (p,), {"lon": west})

    def means_east(p):
        return remote(table.at[1, 1, piece(p)], table.at[1, 0, piece(p)], meast_sem, (p,), {"lon": east})

    def means_up(s, p):
        return remote(table.at[1, s, piece(p)], table.at[0, s, piece(p)], mup_sem, (s, p), {"lat": up})

    def means_down(s, p):
        return remote(table.at[1, s, piece(p)], table.at[2, s, piece(p)], mdown_sem, (s, p), {"lat": down})

    def tally_up():
        return remote(tallies.at[2, :, pl.ds(0, 24)], tally_below, tally_sem, (0,), {"lat": up})

    def tally_down():
        return remote(tallies.at[0, :, pl.ds(0, 24)], tally_above, tally_sem, (1,), {"lat": down})

    def tally_west():
        return remote(tally_middle.at[:, pl.ds(0, 8)], tally_right, tally_sem, (2,), {"lon": west})

    def tally_east():
        return remote(tally_middle.at[:, pl.ds(16, 8)], tally_left, tally_sem, (3,), {"lon": east})

    order = [(s, p) for p in range(PIECES) for s in (0, 2)] + [(1, p) for p in range(PIECES)]

    @pl.when(has_up)
    def _():
        tally_up().start()
        for s, p in order:
            sums_up(s, p).start()

    @pl.when(has_down)
    def _():
        tally_down().start()
        for s, p in order:
            sums_down(s, p).start()

    @pl.when(jnp.logical_not(has_down))
    def _():
        below[...] = jnp.zeros_like(below)
        tally_below[...] = jnp.zeros_like(tally_below)
        table[0] = jnp.zeros_like(table[0])

    @pl.when(jnp.logical_not(has_up))
    def _():
        above[...] = jnp.zeros_like(above)
        tally_above[...] = jnp.zeros_like(tally_above)
        table[2] = jnp.zeros_like(table[2])

    add_up(1)
    high2[...], low1[...] = pairs_of(rates_ref[...])
    chem[...] = chem_ref[...]

    def chemistry(substeps):
        @pl.loop(0, substeps)
        def _(_):
            substep(chem, high2, low1)

    chemistry(EARLY)

    def strips(first, rows, body):
        @pl.loop(0, rows // 8, unroll=4)
        def _(i):
            body(pl.multiple_of(i * 8, 8) + first)

    def bands_summed(s, p):
        @pl.when(has_down)
        def _():
            sums_up(s, p).wait_recv()

        @pl.when(has_up)
        def _():
            sums_down(s, p).wait_recv()

        def add_bands(i):
            part = pl.ds(i, 8)
            middle[s, part, :] = sums_ref[1, s, part, :] + below[s, part, :] + above[s, part, :]

        strips(p * PIECE, PIECE, add_bands)

    def sides_summed(p):
        if p == 0:
            @pl.when(has_down)
            def _():
                tally_up().wait_recv()

            @pl.when(has_up)
            def _():
                tally_down().wait_recv()

            tally_middle[...] = tallies[1, :, 0:24] + tally_below[...] + tally_above[...]
            tally_west().start()
            tally_east().start()
        bands_summed(0, p)
        sums_west(p).start()
        bands_summed(2, p)
        sums_east(p).start()

    def own_summed(p):
        bands_summed(1, p)

    def sectors_summed(p):
        if p == 0:
            tally_west().wait_recv()
            tally_east().wait_recv()
            tally = tally_middle[:, 8:16] + tally_left[...] + tally_right[...]
            inverse = (1.0 / jnp.maximum(tally, 1.0)).reshape(16, LANES)
            factors[...] = jnp.concatenate([inverse, jnp.zeros((LANES - 16, LANES), F32)], 0).T
        sums_west(p).wait_recv()
        sums_east(p).wait_recv()
        q = p * PIECE // QUARTER

        def mean(i):
            part = pl.ds(i, 8)
            factor = factors[pl.ds(i - q * QUARTER, 8), :]
            low = jnp.where(spare, factor[:, 3:4], factor[:, q:q + 1])
            high = jnp.where(spare, factor[:, 11:12], factor[:, 8 + q:9 + q])
            total = middle[1, part, :] + left[part, :] + right[part, :]
            table[1, 1, part, :] = total * jnp.where(lane < 64, low, high)

        strips(p * PIECE, PIECE, mean)
        means_west(p).start()
        means_east(p).start()

        @pl.when(has_up)
        def _():
            means_up(1, p).start()

        @pl.when(has_down)
        def _():
            means_down(1, p).start()

    def means_passed(p):
        means_west(p).wait_recv()
        means_east(p).wait_recv()

        @pl.when(has_up)
        def _():
            means_up(0, p).start()
            means_up(2, p).start()

        @pl.when(has_down)
        def _():
            means_down(0, p).start()
            means_down(2, p).start()

    parts = {"a": sides_summed, "o": own_summed, "b": sectors_summed, "c": means_passed}
    for entry in PLAN:
        if isinstance(entry, int):
            chemistry(entry)
        else:
            parts[entry[0]](entry[1])

    if not last:
        blank_strips(blanks)
    for b in range(BLK):
        column = b % HALF_BLK * LANES
        reacted[b] = chem[b // HALF_BLK, :, column:column + LANES]

    def means_landed(sectors):
        @pl.when(has_up)
        def _():
            for s, p in order:
                if s in sectors:
                    means_down(s, p).wait_recv()

        @pl.when(has_down)
        def _():
            for s, p in order:
                if s in sectors:
                    means_up(s, p).wait_recv()

    def unpack_regions(regions):
        def unpack(i):
            for r, s in regions:
                found = [pltpu.roll(table[r, s, pl.ds(q * QUARTER + i, 8), :], LANES - S + 16 * q, 1) for q in range(3)]
                table[r, s, pl.ds(PACKED + i, 8), :] = jnp.where(spot < 16, found[0], jnp.where(spot < 32, found[1], found[2]))

        strips(0, QUARTER, unpack)

    unpack_regions([(1, 0), (1, 1), (1, 2)])
    means_landed((1,))
    unpack_regions([(0, 1), (2, 1)])
    means_landed((0, 2))
    unpack_regions([(0, 0), (0, 2), (2, 0), (2, 2)])

    mix = jnp.broadcast_to(mix_ref[...], (LANES, S)).T
    flat = table.reshape(9 * ROWS, LANES)

    def gather(b, rows):
        for k in range(LANES):
            rows[k:k + 1, :] = flat[pl.ds(row_ref[step, b, k], 1), :]

    def mixed(b, rows):
        means = rows[...].T
        low = low_ref[step, pl.ds(b, 1), :] == 1
        picked = jnp.where(low, means[0:S], means[64:64 + S])
        return reacted[b] + mix * (picked - moved_ref[b])

    def pair(order_of, target, i):
        first, second = order_of(2 * i), order_of(2 * i + 1)
        gather(first, even)
        gather(second, odd)
        target[2 * i] = mixed(first, even)
        target[2 * i + 1] = mixed(second, odd)

    @pl.when(has_up)
    def _():
        tally_up().wait_send()
        for s, p in order:
            sums_up(s, p).wait_send()
            means_up(s, p).wait_send()

    @pl.when(has_down)
    def _():
        tally_down().wait_send()
        for s, p in order:
            sums_down(s, p).wait_send()
            means_down(s, p).wait_send()

    tally_west().wait_send()
    tally_east().wait_send()
    for p in range(PIECES):
        for copy in (sums_west(p), sums_east(p), means_west(p), means_east(p)):
            copy.wait_send()

    if last:
        @pl.loop(0, BLK // 4, unroll=2)
        def _(i):
            for k, rows in enumerate((even, odd, third, fourth)):
                gather(4 * i + k, rows)
            for k, rows in enumerate((even, odd, third, fourth)):
                out_ref[4 * i + k] = mixed(4 * i + k, rows)
    else:
        polar = is_polar()
        half_unit = jnp.where(polar, 2, 1)

        @pl.loop(0, 6)
        def _(k):
            @pl.loop(0, half_unit)
            def _(u):
                pair(lambda at: order_ref[at], pool, k * half_unit + u)

            for batch in range(6):
                @pl.when(k == batch)
                def _():
                    each_unit(polar, lambda unit: batch_copy(pool, send_sem, recv_sem, batch, unit).start())

        @pl.loop(6 * half_unit, BLK // 2)
        def _(i):
            pair(lambda at: order_ref[at], pool, i)

        def wait(unit):
            for k in range(6):
                batch_copy(pool, send_sem, recv_sem, k, unit).wait()

        each_unit(polar, wait)

        @pl.loop(0, BLK, unroll=4)
        def _(slot):
            out_ref[slot] = pool[source_ref[slot]]


def exchange(step, sums, moved, chem, rates, mix, low, row, order, source):
    region = pltpu.VMEM((3, PACKED, LANES), F32)
    beside = pltpu.VMEM((PACKED, LANES), F32)
    tally = pltpu.VMEM((2, 24, LANES), F32)
    tally_beside = pltpu.VMEM((2, 8, LANES), F32)
    square = pltpu.VMEM((LANES, LANES), F32)
    pair = pltpu.SemaphoreType.DMA((2, 3, PIECES))
    single = pltpu.SemaphoreType.DMA((2, PIECES))
    blanks = 0 if step == STEPS - 1 else ACCS
    state = jax.ShapeDtypeStruct((BLK, S, LANES), F32)
    return pl.pallas_call(
        functools.partial(exchange_kernel, step),
        out_shape=(state,) + (TABLE,) * blanks,
        in_specs=[VMEM, VMEM, VMEM, VMEM, VMEM, SMEM, SMEM, SMEM] + [VMEM] * ACCS,
        out_specs=(VMEM,) * (1 + blanks),
        scratch_shapes=[
            pltpu.VMEM((3, 3, PACKED, LANES), F32),
            square,
            pltpu.VMEM((3, 2, 64, LANES), F32),
            region, region, tally, tally, region, tally,
            beside, beside, tally_beside, tally_beside,
            square,
            pltpu.VMEM((3, 3, ROWS, LANES), F32),
            pltpu.VMEM((2, S, BLK // 2 * LANES), F32),
            pltpu.VMEM((2 * S, 4 * S), BF16),
            pltpu.VMEM((2 * S, 2 * S), BF16),
            square, square, square, square,
            pltpu.VMEM((BLK, S, LANES), F32),
            pltpu.VMEM((2 * BLK, S, LANES), F32),
            pair, pair, single, single, single, single, pair, pair,
            pltpu.SemaphoreType.DMA((2, 4)),
            pltpu.SemaphoreType.DMA((6,)),
            pltpu.SemaphoreType.DMA((6,)),
        ],
        compiler_params=pltpu.CompilerParams(collective_id=2 + step, has_side_effects=True, vmem_limit_bytes=LIMIT),
        name="exchange",
    )(moved, chem, rates, mix, low, row, order, source, *sums)


def shards(species, reaction_rates, mix_rate, shift_list, arrival, cell_index):
    inputs = (shift_list, arrival, species, cell_index, reaction_rates, mix_rate.reshape(1, S))
    inputs = (pltpu.with_memory_space_constraint(x, pltpu.HBM) for x in inputs)
    moved, row, low, place, source, rates, mix, *accs = migrate(*inputs)
    for step in range(STEPS):
        sums, order, chem = deposit(step, moved, low, row, place, rates, accs)
        moved, *accs = exchange(step, sums, moved, chem, rates, mix, low, row, order, source)
    return moved


def solution(mesh):
    placed = (
        P(("lat", "lon"), None, None),
        P(),
        P(),
        P(None, "lat", None),
        P(None, ("lat", "lon")),
        P(None, ("lat", "lon"), None),
    )
    return jax.shard_map(
        shards, mesh=mesh, in_specs=placed, out_specs=P(("lat", "lon"), None, None), check_vma=False
    )
```

```python
import functools

import jax
import jax.numpy as jnp
from jax import lax
from jax.experimental import pallas as pl
from jax.experimental.pallas import tpu as pltpu
from jax.sharding import PartitionSpec as P

S = 48
LANES = 128
BLK = 32
HALF_BLK = BLK // 2
CELL_DEV = 1024
ROWS = CELL_DEV // 2
STEPS = 2
SUB = 32
ACCS = 6
QUARTER = ROWS // 4
PACKED = 3 * QUARTER
PIECES = 6
PIECE = PACKED // PIECES
F32 = jnp.float32
BF16 = jnp.bfloat16
MESH = pl.DeviceIdType.MESH
VMEM = pl.BlockSpec(memory_space=pltpu.VMEM)
SMEM = pl.BlockSpec(memory_space=pltpu.SMEM)
HBM = pl.BlockSpec(memory_space=pltpu.HBM)
TABLE = jax.ShapeDtypeStruct((9 * ROWS, LANES), F32)
LIMIT = 24 * 2**20
BATCHES = (2, -2, 1, 1, -1, -1)
FIRST = {2: 0, -2: 1, 1: 2, -1: 4}
PLAN = (
    ("a", 0), 1, ("a", 1), 1, ("a", 2), 1, ("a", 3), 1, ("a", 4), 1, ("a", 5), 1,
    ("o", 0), ("b", 0), ("o", 1), ("b", 1), 1, ("o", 2), ("b", 2), ("o", 3), ("b", 3), 1, ("o", 4), ("b", 4), ("o", 5), ("b", 5),
    ("z", 0), 3, ("c", 0), 1, ("c", 1), 1, ("c", 2), 1, ("c", 3), 1, ("c", 4), 1, ("c", 5), 4,
)
EARLY = 4


def around(axis, step):
    count = lax.axis_size(axis)
    return lax.rem(lax.axis_index(axis) + step + count, count)


def is_polar():
    band = lax.axis_index("lat")
    return (band == 0) | (band == lax.axis_size("lat") - 1)


def place_slots(shift_ref, step, unit, visit):
    def place(slot, counts):
        moved_by = shift_ref[step, 0, slot]
        where = 6 * unit + counts[4]
        later = []
        for offset, count in zip((2, -2, 1, -1), counts):
            hit = moved_by == offset
            where = jnp.where(hit, FIRST[offset] * unit + count, where)
            later.append(count + hit.astype(jnp.int32))
        later.append(counts[4] + (moved_by == 0).astype(jnp.int32))
        visit(slot, moved_by, jnp.minimum(where, BLK - 1))
        return tuple(later)

    lax.fori_loop(0, BLK, place, (jnp.int32(0),) * 5)


def batch_copy(pool, send_sem, recv_sem, k, unit):
    return pltpu.make_async_remote_copy(
        src_ref=pool.at[pl.ds(k * unit, unit)],
        dst_ref=pool.at[pl.ds(BLK + k * unit, unit)],
        send_sem=send_sem.at[k],
        recv_sem=recv_sem.at[k],
        device_id={"lon": around("lon", BATCHES[k])},
        device_id_type=MESH,
    )


def each_unit(polar, body):
    @pl.when(polar)
    def _():
        body(4)

    @pl.when(jnp.logical_not(polar))
    def _():
        body(2)


def blank_strips(refs):
    blank = jnp.zeros((8, LANES), F32)

    @pl.loop(0, 9 * ROWS // 8, unroll=4)
    def _(i):
        part = pl.ds(pl.multiple_of(i * 8, 8), 8)
        for ref in refs:
            ref[part, :] = blank


def migrate_kernel(
    shift_hbm, arrival_hbm, state_hbm, cell_hbm, rates_hbm, mix_hbm,
    moved_ref, row_ref, low_ref, place_ref, source_ref, rates_ref, mix_ref, *rest
):
    accs = rest[:ACCS]
    shift_ref, arrival_ref, state_ref, cell_ref, pool, pool_at, load_sem, send_sem, recv_sem = rest[ACCS:]
    loads = [
        pltpu.make_async_copy(src, dst, load_sem.at[k])
        for k, (src, dst) in enumerate(
            (
                (shift_hbm, shift_ref), (arrival_hbm, arrival_ref), (state_hbm, state_ref), (cell_hbm, cell_ref),
                (rates_hbm, rates_ref), (mix_hbm, mix_ref),
            )
        )
    ]
    for load in loads:
        load.start()
    polar = is_polar()
    unit = jnp.where(polar, 4, 2)
    barrier = pltpu.get_barrier_semaphore()
    for offset in (1, -1, 2, -2):
        pl.semaphore_signal(barrier, inc=1, device_id={"lon": around("lon", offset)}, device_id_type=MESH)

    def note(slot, moved_by, where):
        pool_at[slot] = where + jnp.where(moved_by == 0, 0, BLK)

    def note_later(slot, moved_by, where):
        place_ref[slot] = where + jnp.where(moved_by == 0, 0, BLK)

    loads[0].wait()
    place_slots(shift_ref, 0, unit, note)
    loads[1].wait()
    loads[2].wait()

    @pl.loop(0, 6 * unit)
    def _(where):
        def seek(slot, found):
            return jnp.where(pool_at[slot] == where + BLK, slot, found)

        pool[where] = state_ref[lax.fori_loop(0, BLK, seek, jnp.int32(0), unroll=True)]

    pl.semaphore_wait(barrier, 4)

    def start(unit):
        for k in range(6):
            batch_copy(pool, send_sem, recv_sem, k, unit).start()

    each_unit(polar, start)
    for load in loads[3:]:
        load.wait()
    sectors = lax.axis_size("lon")
    cell = cell_ref[...]
    owner = cell // CELL_DEV
    rel_band = owner // sectors - lax.axis_index("lat") + 1
    rel_sector = (owner % sectors - lax.axis_index("lon") + 1 + sectors) % sectors
    row_ref[...] = jnp.clip((rel_band * 3 + rel_sector) * ROWS + cell % ROWS, 0, 9 * ROWS - 1)
    low_ref[...] = 1 - cell // ROWS % 2
    place_slots(shift_ref, STEPS - 1, unit, note_later)

    @pl.loop(0, BLK)
    def _(slot):
        source_ref[slot] = place_ref[arrival_ref[STEPS - 1, slot]]

    blank_strips(accs)

    def wait(unit):
        for k in range(6):
            batch_copy(pool, send_sem, recv_sem, k, unit).wait()

    each_unit(polar, wait)

    @pl.loop(0, BLK, unroll=4)
    def _(slot):
        old = arrival_ref[0, slot]
        at = pool_at[old]
        moved_ref[slot] = jnp.where(at < BLK, state_ref[old], pool[at])


def migrate(shift_list, arrival, state, cell_index, rates, mix):
    whole = jax.ShapeDtypeStruct((STEPS, BLK, LANES), jnp.int32)
    slots = jax.ShapeDtypeStruct((BLK,), jnp.int32)
    return pl.pallas_call(
        migrate_kernel,
        out_shape=(jax.ShapeDtypeStruct((BLK, S, LANES), F32), whole, whole, slots, slots)
        + (jax.ShapeDtypeStruct((S, S), F32), jax.ShapeDtypeStruct((1, S), F32))
        + (TABLE,) * ACCS,
        in_specs=[HBM] * 6,
        out_specs=(VMEM, VMEM, VMEM, SMEM, SMEM, VMEM, VMEM) + (VMEM,) * ACCS,
        scratch_shapes=[
            pltpu.SMEM((STEPS, 1, BLK), jnp.int32),
            pltpu.SMEM((STEPS, BLK), jnp.int32),
            pltpu.VMEM((BLK, S, LANES), F32),
            pltpu.VMEM((STEPS, BLK, LANES), jnp.int32),
            pltpu.VMEM((2 * BLK, S, LANES), F32),
            pltpu.SMEM((BLK,), jnp.int32),
            pltpu.SemaphoreType.DMA((6,)),
            pltpu.SemaphoreType.DMA((6,)),
            pltpu.SemaphoreType.DMA((6,)),
        ],
        compiler_params=pltpu.CompilerParams(collective_id=1, has_side_effects=True, vmem_limit_bytes=LIMIT),
        name="migrate",
    )(shift_list, arrival, state, cell_index, rates, mix)


def split(x):
    high = x.astype(BF16)
    return high, (x - high.astype(F32)).astype(BF16)


def pairs_of(rates):
    zero = jnp.zeros((S, S), F32)
    high, low = split(jnp.concatenate([jnp.concatenate([rates, zero], 1), jnp.concatenate([zero, rates], 1)], 0))
    return jnp.concatenate([high, high], 1), low


def substep(chem, high2, low1):
    state = chem[...].reshape(2 * S, HALF_BLK * LANES)
    high, low = split(state)
    pushed = jnp.dot(high2[...], jnp.concatenate([high, low], 0), preferred_element_type=F32)
    pushed = pushed + jnp.dot(low1[...], high, preferred_element_type=F32)
    chem[...] = (state + (2.0 / SUB) * jnp.tanh(pushed)).reshape(2, S, HALF_BLK * LANES)


def deposit_kernel(step, moved_ref, low_ref, row_ref, place_ref, rates_ref, *rest):
    accs = rest[ACCS:2 * ACCS]
    order_ref, chem, even, odd, high2, low1 = rest[2 * ACCS:]
    high2[...], low1[...] = pairs_of(rates_ref[...])
    for b in range(BLK):
        column = b % HALF_BLK * LANES
        chem[b // HALF_BLK, :, column:column + LANES] = moved_ref[b]
    tail = jnp.where(lax.broadcasted_iota(jnp.int32, (16, LANES), 0) == 0, 1.0, 0.0)

    def turn(b, rows):
        block = jnp.concatenate([moved_ref[b], tail], 0)
        low = low_ref[step, pl.ds(b, 1), :] == 1
        rows[...] = jnp.concatenate([jnp.where(low, block, 0.0), jnp.where(low, 0.0, block)], 0).T

    def add(b, rows):
        for k in range(LANES):
            acc = accs[k % ACCS]
            at = pl.ds(row_ref[step, b, k], 1)
            acc[at, :] = acc[at, :] + rows[k:k + 1, :]

    turn(0, even)

    @pl.loop(0, BLK // 4)
    def _(i):
        substep(chem, high2, low1)
        turn(4 * i + 1, odd)
        add(4 * i, even)
        turn(4 * i + 2, even)
        add(4 * i + 1, odd)
        turn(4 * i + 3, odd)
        add(4 * i + 2, even)
        turn(jnp.minimum(4 * i + 4, BLK - 1), even)
        add(4 * i + 3, odd)

    @pl.loop(0, BLK)
    def _(slot):
        order_ref[place_ref[slot] % BLK] = slot


def deposit(step, moved, low, row, place, rates, accs):
    *sums, order, chem = pl.pallas_call(
        functools.partial(deposit_kernel, step),
        out_shape=(TABLE,) * ACCS
        + (jax.ShapeDtypeStruct((BLK,), jnp.int32), jax.ShapeDtypeStruct((2, S, HALF_BLK * LANES), F32)),
        in_specs=[VMEM, VMEM, SMEM, SMEM, VMEM] + [VMEM] * ACCS,
        out_specs=(VMEM,) * ACCS + (SMEM, VMEM),
        input_output_aliases={5 + k: k for k in range(ACCS)},
        scratch_shapes=[
            pltpu.VMEM((LANES, LANES), F32),
            pltpu.VMEM((LANES, LANES), F32),
            pltpu.VMEM((2 * S, 4 * S), BF16),
            pltpu.VMEM((2 * S, 2 * S), BF16),
        ],
        compiler_params=pltpu.CompilerParams(vmem_limit_bytes=LIMIT),
        name="deposit",
    )(moved, low, row, place, rates, *accs)
    return sums, order, chem


def exchange_kernel(
    step, moved_ref, chem_ref, rates_ref, mix_ref, low_ref, row_ref, order_ref, source_ref, *rest
):
    last = step == STEPS - 1
    accs = rest[:ACCS]
    out_ref = rest[ACCS]
    blanks = () if last else rest[ACCS + 1:2 * ACCS + 1]
    (
        sums_ref, counts, tallies, below, above, tally_below, tally_above, middle, tally_middle,
        left, right, tally_left, tally_right, factors, table, chem, high2, low1, even, odd, third, fourth, reacted, pool,
        up_sem, down_sem, west_sem, east_sem, mwest_sem, meast_sem, mup_sem, mdown_sem, tally_sem, send_sem, recv_sem,
    ) = rest[ACCS + 1 + len(blanks):]
    lane = lax.broadcasted_iota(jnp.int32, (8, LANES), 1)
    spot = lane % 64
    spare = spot >= S
    def add_up(r):
        @pl.loop(0, QUARTER // 8, unroll=4)
        def _(i):
            at = pl.multiple_of(i * 8, 8)
            tally = jnp.zeros((8, LANES), F32)
            for s in range(3):
                quarters = []
                for q in range(4):
                    part = pl.ds((r * 3 + s) * ROWS + q * QUARTER + at, 8)
                    total = accs[0][part, :]
                    for acc in accs[1:]:
                        total = total + acc[part, :]
                    quarters.append(total)
                    tally = jnp.where(spot == s * 8 + q, pltpu.roll(total, (s * 8 + q - S) % LANES, 1), tally)
                for q in range(3):
                    sums_ref[r, s, pl.ds(q * QUARTER + at, 8), :] = jnp.where(
                        spare, pltpu.roll(quarters[3], S - 16 * q, 1), quarters[q]
                    )
            counts[pl.ds(at, 8), :] = tally

        tallies[r] = counts[...].T.reshape(2, 64, LANES)

    band = lax.axis_index("lat")
    bands = lax.axis_size("lat")
    has_up = band < bands - 1
    has_down = band > 0
    up = jnp.minimum(band + 1, bands - 1)
    down = jnp.maximum(band - 1, 0)
    east = around("lon", 1)
    west = around("lon", -1)
    beside = (1, -1) if last else (1, -1, 2, -2)
    barrier = pltpu.get_barrier_semaphore()
    for offset in beside:
        pl.semaphore_signal(barrier, inc=1, device_id={"lon": around("lon", offset)}, device_id_type=MESH)

    @pl.when(has_up)
    def _():
        pl.semaphore_signal(barrier, inc=1, device_id={"lat": up}, device_id_type=MESH)

    @pl.when(has_down)
    def _():
        pl.semaphore_signal(barrier, inc=1, device_id={"lat": down}, device_id_type=MESH)

    add_up(2)
    add_up(0)
    pl.semaphore_wait(barrier, len(beside) + has_up.astype(jnp.int32) + has_down.astype(jnp.int32))

    def remote(src, dst, sem, index, device):
        return pltpu.make_async_remote_copy(
            src_ref=src, dst_ref=dst, send_sem=sem.at[(0,) + index], recv_sem=sem.at[(1,) + index],
            device_id=device, device_id_type=MESH,
        )

    def piece(p):
        return pl.ds(p * PIECE, PIECE)

    def sums_up(s, p):
        return remote(sums_ref.at[2, s, piece(p)], below.at[s, piece(p)], up_sem, (s, p), {"lat": up})

    def sums_down(s, p):
        return remote(sums_ref.at[0, s, piece(p)], above.at[s, piece(p)], down_sem, (s, p), {"lat": down})

    def sums_west(p):
        return remote(middle.at[0, piece(p)], right.at[piece(p)], west_sem, (p,), {"lon": west})

    def sums_east(p):
        return remote(middle.at[2, piece(p)], left.at[piece(p)], east_sem, (p,), {"lon": east})

    def means_west(p):
        return remote(table.at[1, 1, piece(p)], table.at[1, 2, piece(p)], mwest_sem, (p,), {"lon": west})

    def means_east(p):
        return remote(table.at[1, 1, piece(p)], table.at[1, 0, piece(p)], meast_sem, (p,), {"lon": east})

    def means_up(s, p):
        return remote(table.at[1, s, piece(p)], table.at[0, s, piece(p)], mup_sem, (s, p), {"lat": up})

    def means_down(s, p):
        return remote(table.at[1, s, piece(p)], table.at[2, s, piece(p)], mdown_sem, (s, p), {"lat": down})

    def tally_up():
        return remote(tallies.at[2, :, pl.ds(0, 24)], tally_below, tally_sem, (0,), {"lat": up})

    def tally_down():
        return remote(tallies.at[0, :, pl.ds(0, 24)], tally_above, tally_sem, (1,), {"lat": down})

    def tally_west():
        return remote(tally_middle.at[:, pl.ds(0, 8)], tally_right, tally_sem, (2,), {"lon": west})

    def tally_east():
        return remote(tally_middle.at[:, pl.ds(16, 8)], tally_left, tally_sem, (3,), {"lon": east})

    order = [(s, p) for p in range(PIECES) for s in (0, 2)] + [(1, p) for p in range(PIECES)]

    @pl.when(has_up)
    def _():
        tally_up().start()
        for s, p in order:
            sums_up(s, p).start()

    @pl.when(has_down)
    def _():
        tally_down().start()
        for s, p in order:
            sums_down(s, p).start()

    @pl.when(jnp.logical_not(has_down))
    def _():
        below[...] = jnp.zeros_like(below)
        tally_below[...] = jnp.zeros_like(tally_below)
        table[0] = jnp.zeros_like(table[0])

    @pl.when(jnp.logical_not(has_up))
    def _():
        above[...] = jnp.zeros_like(above)
        tally_above[...] = jnp.zeros_like(tally_above)
        table[2] = jnp.zeros_like(table[2])

    add_up(1)
    high2[...], low1[...] = pairs_of(rates_ref[...])
    chem[...] = chem_ref[...]

    def chemistry(substeps):
        @pl.loop(0, substeps)
        def _(_):
            substep(chem, high2, low1)

    chemistry(EARLY)

    def strips(first, rows, body):
        @pl.loop(0, rows // 8, unroll=4)
        def _(i):
            body(pl.multiple_of(i * 8, 8) + first)

    def bands_summed(s, p):
        @pl.when(has_down)
        def _():
            sums_up(s, p).wait_recv()

        @pl.when(has_up)
        def _():
            sums_down(s, p).wait_recv()

        def add_bands(i):
            part = pl.ds(i, 8)
            middle[s, part, :] = sums_ref[1, s, part, :] + below[s, part, :] + above[s, part, :]

        strips(p * PIECE, PIECE, add_bands)

    def sides_summed(p):
        if p == 0:
            @pl.when(has_down)
            def _():
                tally_up().wait_recv()

            @pl.when(has_up)
            def _():
                tally_down().wait_recv()

            tally_middle[...] = tallies[1, :, 0:24] + tally_below[...] + tally_above[...]
            tally_west().start()
            tally_east().start()
        bands_summed(0, p)
        sums_west(p).start()
        bands_summed(2, p)
        sums_east(p).start()

    def own_summed(p):
        bands_summed(1, p)

    def sectors_summed(p):
        if p == 0:
            tally_west().wait_recv()
            tally_east().wait_recv()
            tally = tally_middle[:, 8:16] + tally_left[...] + tally_right[...]
            inverse = (1.0 / jnp.maximum(tally, 1.0)).reshape(16, LANES)
            factors[...] = jnp.concatenate([inverse, jnp.zeros((LANES - 16, LANES), F32)], 0).T
        sums_west(p).wait_recv()
        sums_east(p).wait_recv()
        q = p * PIECE // QUARTER

        def mean(i):
            part = pl.ds(i, 8)
            factor = factors[pl.ds(i - q * QUARTER, 8), :]
            low = jnp.where(spare, factor[:, 3:4], factor[:, q:q + 1])
            high = jnp.where(spare, factor[:, 11:12], factor[:, 8 + q:9 + q])
            total = middle[1, part, :] + left[part, :] + right[part, :]
            table[1, 1, part, :] = total * jnp.where(lane < 64, low, high)

        strips(p * PIECE, PIECE, mean)
        means_west(p).start()
        means_east(p).start()

        @pl.when(has_up)
        def _():
            means_up(1, p).start()

        @pl.when(has_down)
        def _():
            means_down(1, p).start()

    def means_passed(p):
        means_west(p).wait_recv()
        means_east(p).wait_recv()

        @pl.when(has_up)
        def _():
            means_up(0, p).start()
            means_up(2, p).start()

        @pl.when(has_down)
        def _():
            means_down(0, p).start()
            means_down(2, p).start()

    parts = {"z": lambda _: blank_strips(blanks) if blanks else None, "a": sides_summed, "o": own_summed, "b": sectors_summed, "c": means_passed}
    for entry in PLAN:
        if isinstance(entry, int):
            chemistry(entry)
        else:
            parts[entry[0]](entry[1])

    for b in range(BLK):
        column = b % HALF_BLK * LANES
        reacted[b] = chem[b // HALF_BLK, :, column:column + LANES]

    def means_landed(sectors):
        @pl.when(has_up)
        def _():
            for s, p in order:
                if s in sectors:
                    means_down(s, p).wait_recv()

        @pl.when(has_down)
        def _():
            for s, p in order:
                if s in sectors:
                    means_up(s, p).wait_recv()

    def unpack_regions(regions):
        def unpack(i):
            for r, s in regions:
                found = [pltpu.roll(table[r, s, pl.ds(q * QUARTER + i, 8), :], LANES - S + 16 * q, 1) for q in range(3)]
                table[r, s, pl.ds(PACKED + i, 8), :] = jnp.where(spot < 16, found[0], jnp.where(spot < 32, found[1], found[2]))

        strips(0, QUARTER, unpack)

    unpack_regions([(1, 0), (1, 1), (1, 2)])
    means_landed((1,))
    unpack_regions([(0, 1), (2, 1)])
    means_landed((0, 2))
    unpack_regions([(0, 0), (0, 2), (2, 0), (2, 2)])

    mix = jnp.broadcast_to(mix_ref[...], (LANES, S)).T
    flat = table.reshape(9 * ROWS, LANES)

    def gather(b, rows):
        for k in range(LANES):
            rows[k:k + 1, :] = flat[pl.ds(row_ref[step, b, k], 1), :]

    def mixed(b, rows):
        means = rows[...].T
        low = low_ref[step, pl.ds(b, 1), :] == 1
        picked = jnp.where(low, means[0:S], means[64:64 + S])
        return reacted[b] + mix * (picked - moved_ref[b])

    def pair(order_of, target, i):
        first, second = order_of(2 * i), order_of(2 * i + 1)
        gather(first, even)
        gather(second, odd)
        target[2 * i] = mixed(first, even)
        target[2 * i + 1] = mixed(second, odd)

    @pl.when(has_up)
    def _():
        tally_up().wait_send()
        for s, p in order:
            sums_up(s, p).wait_send()
            means_up(s, p).wait_send()

    @pl.when(has_down)
    def _():
        tally_down().wait_send()
        for s, p in order:
            sums_down(s, p).wait_send()
            means_down(s, p).wait_send()

    tally_west().wait_send()
    tally_east().wait_send()
    for p in range(PIECES):
        for copy in (sums_west(p), sums_east(p), means_west(p), means_east(p)):
            copy.wait_send()

    if last:
        @pl.loop(0, BLK // 4)
        def _(i):
            for k, rows in enumerate((even, odd, third, fourth)):
                gather(4 * i + k, rows)
            for k, rows in enumerate((even, odd, third, fourth)):
                out_ref[4 * i + k] = mixed(4 * i + k, rows)
    else:
        polar = is_polar()
        half_unit = jnp.where(polar, 2, 1)

        @pl.loop(0, 6)
        def _(k):
            @pl.loop(0, half_unit)
            def _(u):
                pair(lambda at: order_ref[at], pool, k * half_unit + u)

            for batch in range(6):
                @pl.when(k == batch)
                def _():
                    each_unit(polar, lambda unit: batch_copy(pool, send_sem, recv_sem, batch, unit).start())

        @pl.loop(6 * half_unit, BLK // 2)
        def _(i):
            pair(lambda at: order_ref[at], pool, i)

        def wait(unit):
            for k in range(6):
                batch_copy(pool, send_sem, recv_sem, k, unit).wait()

        each_unit(polar, wait)

        @pl.loop(0, BLK, unroll=4)
        def _(slot):
            out_ref[slot] = pool[source_ref[slot]]


def exchange(step, sums, moved, chem, rates, mix, low, row, order, source):
    region = pltpu.VMEM((3, PACKED, LANES), F32)
    beside = pltpu.VMEM((PACKED, LANES), F32)
    tally = pltpu.VMEM((2, 24, LANES), F32)
    tally_beside = pltpu.VMEM((2, 8, LANES), F32)
    square = pltpu.VMEM((LANES, LANES), F32)
    pair = pltpu.SemaphoreType.DMA((2, 3, PIECES))
    single = pltpu.SemaphoreType.DMA((2, PIECES))
    blanks = 0 if step == STEPS - 1 else ACCS
    state = jax.ShapeDtypeStruct((BLK, S, LANES), F32)
    return pl.pallas_call(
        functools.partial(exchange_kernel, step),
        out_shape=(state,) + (TABLE,) * blanks,
        in_specs=[VMEM, VMEM, VMEM, VMEM, VMEM, SMEM, SMEM, SMEM] + [VMEM] * ACCS,
        out_specs=(VMEM,) * (1 + blanks),
        scratch_shapes=[
            pltpu.VMEM((3, 3, PACKED, LANES), F32),
            square,
            pltpu.VMEM((3, 2, 64, LANES), F32),
            region, region, tally, tally, region, tally,
            beside, beside, tally_beside, tally_beside,
            square,
            pltpu.VMEM((3, 3, ROWS, LANES), F32),
            pltpu.VMEM((2, S, BLK // 2 * LANES), F32),
            pltpu.VMEM((2 * S, 4 * S), BF16),
            pltpu.VMEM((2 * S, 2 * S), BF16),
            square, square, square, square,
            pltpu.VMEM((BLK, S, LANES), F32),
            pltpu.VMEM((2 * BLK, S, LANES), F32),
            pair, pair, single, single, single, single, pair, pair,
            pltpu.SemaphoreType.DMA((2, 4)),
            pltpu.SemaphoreType.DMA((6,)),
            pltpu.SemaphoreType.DMA((6,)),
        ],
        compiler_params=pltpu.CompilerParams(collective_id=2 + step, has_side_effects=True, vmem_limit_bytes=LIMIT),
        name="exchange",
    )(moved, chem, rates, mix, low, row, order, source, *sums)


def shards(species, reaction_rates, mix_rate, shift_list, arrival, cell_index):
    inputs = (shift_list, arrival, species, cell_index, reaction_rates, mix_rate.reshape(1, S))
    inputs = (pltpu.with_memory_space_constraint(x, pltpu.HBM) for x in inputs)
    moved, row, low, place, source, rates, mix, *accs = migrate(*inputs)
    for step in range(STEPS):
        sums, order, chem = deposit(step, moved, low, row, place, rates, accs)
        moved, *accs = exchange(step, sums, moved, chem, rates, mix, low, row, order, source)
    return moved


def solution(mesh):
    placed = (
        P(("lat", "lon"), None, None),
        P(),
        P(),
        P(None, "lat", None),
        P(None, ("lat", "lon")),
        P(None, ("lat", "lon"), None),
    )
    return jax.shard_map(
        shards, mesh=mesh, in_specs=placed, out_specs=P(("lat", "lon"), None, None), check_vma=False
    )
```
